512 devices in a mesh: frame: 4 (over x), row: 16 (over z_hi, y), col: 8 (over z_lo, core).
Axes of the slice: x: 4, y: 4, z: 16 (z_hi: 4, z_lo: 4; z = z_hi * 4 + z_lo), core: 2. Of those that a mesh axis runs over, the one named last changes fastest.
Arguments:
- object_field: float32 [4096, 4096], P('row', 'col'), may hold values from -6 to 6
- images: float32 [4, 4096, 4096], P('frame', 'row', 'col'), may hold values from -6 to 6
- transfer_real: float32 [4, 4096, 4096], P('frame', ('row', 'col')), may hold values from -6 to 6
- transfer_imaginary: float32 [4, 4096, 4096], P('frame', ('row', 'col')), may hold values from -6 to 6
Outputs:
- gradient: float32 [4096, 4096], P(('frame', 'row'), 'col')
The draws below stay inside these ranges and needn't reach their ends.
All inputs are finite; a program needn't handle non-finite values.
Results may differ from the reference program's by a relative error of at most 0.00011.
Values sent between devices are 32-bit elements; how exact they have to be, the bound alone decides.
A program may use at most 64 MiB of HBM per device.

```python
import jax
import jax.numpy as jnp
from jax import lax

N = 4096
FRAMES = 4


def steps_of(key, extent, pieces, smallest, high):
    loudness, own = 1.0, jax.random.fold_in(key, 6)
    for position, blocks in pieces:
        draws = jnp.exp(jax.random.uniform(jax.random.fold_in(own, position), (blocks,), jnp.float32, smallest / len(pieces), high / len(pieces)))
        loudness = loudness * jnp.repeat(draws, extent[position] // blocks).reshape([-1 if axis == position else 1 for axis in range(len(extent))])
    return loudness


def bell_draw(key, dims, width, most, pieces=(), held_as=jnp.bfloat16):
    entries = jax.random.normal(key, dims, jnp.float32) * width
    if len(pieces) > 0:
        entries = steps_of(key, dims, pieces, -0.22, 0.18) * entries
    return jnp.clip(entries, min=-most, max=most).astype(held_as)


def setup_inputs(seed: int = 0) -> dict:
    splits = jax.random.split(jax.random.key(seed), 5)
    return {
        "object_field": bell_draw(splits[0], (N, N), 1.0, 6.0, ((0, 16), (1, 8)), jnp.float32),
        "images": bell_draw(splits[1], (FRAMES, N, N), 1.0, 6.0, ((0, 4), (1, 16), (2, 8)), jnp.float32),
        "transfer_real": bell_draw(splits[2], (FRAMES, N, N), 0.7, 6.0, ((0, 4), (1, 128)), jnp.float32),
        "transfer_imaginary": bell_draw(splits[3], (FRAMES, N, N), 0.7, 6.0, ((0, 4), (1, 128)), jnp.float32),
    }


def reference(object_field, images, transfer_real, transfer_imaginary):
    spectrum = jnp.fft.fft2(object_field)

    def add_frame(summed, frame_data):
        exposure, coefficients_real, coefficients_imaginary = frame_data
        transfer = lax.complex(coefficients_real, coefficients_imaginary).T
        modelled = jnp.real(jnp.fft.ifft2(transfer * spectrum))
        weighted = (modelled - exposure) / (0.5 + jnp.abs(exposure))
        adjoint = jnp.conj(transfer) * jnp.fft.fft2(weighted)
        return summed + adjoint, None

    summed, unused = lax.scan(add_frame, jnp.zeros_like(spectrum), (images, transfer_real, transfer_imaginary))
    return jnp.real(jnp.fft.ifft2(summed))
```

```python
import functools
import math

import jax
import jax.numpy as jnp
import ml_dtypes
import numpy as np
from jax import lax
from jax.experimental import pallas as pl
from jax.experimental.pallas import tpu as pltpu
from jax.sharding import PartitionSpec as P

F32 = jnp.float32
BF16 = jnp.bfloat16
MESH = pl.DeviceIdType.MESH

N = 4096
DEVICES = 128


def block_of(g):
    return np.where(g < 64, 2 * g, 2 * (127 - g) + 1)


def halves(table):
    high = table.astype(np.float32).astype(ml_dtypes.bfloat16)
    low = (table - high.astype(np.float64)).astype(np.float32).astype(ml_dtypes.bfloat16)
    return high, low


def turn(numbers, length):
    angles = 2.0 * math.pi / length * (numbers % length)
    return np.cos(angles), np.sin(angles)


def vertical_forward(order):
    cosine, sine = turn(np.arange(512)[:, None] * order[None, :], 512)
    pieces = []
    for chunk in range(4):
        rows = slice(128 * chunk, 128 * chunk + 128)
        high, low = halves(np.concatenate([cosine[rows], -sine[rows]], 0))
        pieces += [high, low]
    return np.concatenate(pieces, 0)


def vertical_inverse(order):
    cosine, sine = turn(order[:, None] * np.arange(512)[None, :], 512)
    whole = np.concatenate([sine, cosine, -sine], 1)
    pieces = []
    for chunk in range(4):
        pieces += list(halves(whole[128 * chunk : 128 * chunk + 128]))
    return np.concatenate(pieces, 0)


def tables():
    made = {}
    g = np.arange(128)
    full = (4 * g[None, :] + np.arange(4)[:, None]).reshape(-1)
    f, r, c = np.meshgrid(np.arange(4), np.arange(16), np.arange(8), indexing="ij")
    made["down_object"] = vertical_forward((32 * r + 8 * f + c).reshape(-1))
    made["down_full"] = vertical_forward(full)
    made["up_full"] = vertical_inverse(full)
    f, c, r = np.meshgrid(np.arange(4), np.arange(8), np.arange(16), indexing="ij")
    made["up_gradient"] = vertical_inverse((128 * f + 8 * r + c).reshape(-1))

    s, t = np.meshgrid(np.arange(16), np.arange(8), indexing="ij")
    s, t = s.reshape(-1), t.reshape(-1)
    sh, v1, sl = np.meshgrid(np.arange(2), np.arange(8), np.arange(8), indexing="ij")
    spectral_s, spectral_v = (8 * sh + sl).reshape(-1), v1.reshape(-1)
    cosine, sine = turn(t[:, None] * spectral_v[None, :], 8)
    same = (s[:, None] == spectral_s[None, :]).astype(np.float64)
    cosine, sine = cosine * same, sine * same
    made["mix_down"] = np.concatenate(halves(np.block([[cosine, -sine], [sine, cosine]])), 0)
    made["mix_up"] = np.concatenate(halves(np.block([[cosine.T, sine.T], [-sine.T, cosine.T]])), 0)
    cosine, sine = turn(np.arange(512)[:, None] * t[None, :], 4096)
    made["twist_vertical"] = np.concatenate([cosine, sine], 0).astype(np.float32)

    x1, tx = s, t
    same = (t[:, None] == tx[None, :]).astype(np.float64)
    cosine, sine = turn(s[:, None] * x1[None, :], 16)
    cosine, sine = cosine * same, sine * same
    made["open_x"] = np.concatenate(halves(np.concatenate([cosine, -sine], 0)), 0)
    scale = 1.0 / (float(N) * float(N))
    made["close_x"] = np.concatenate(halves(np.concatenate([cosine.T, -sine.T], 1) * scale), 0)
    cosine, sine = turn(s[:, None] * np.arange(256)[None, :], 4096)
    made["twist_out"] = np.concatenate([cosine, sine], 0).astype(np.float32)
    made["twist_in"] = np.concatenate([cosine.T, sine.T], 0).astype(np.float32)

    def across(order):
        cosine, sine = turn(block_of(order)[:, None] * np.arange(256)[None, :], 256)
        alternate = np.zeros((16, 512))
        alternate[0, :256] = 1.0 - 2.0 * (np.arange(256) % 2)
        whole = np.concatenate(
            [np.concatenate([cosine, sine], 1), np.concatenate([-sine, cosine], 1), alternate], 0
        )
        return np.concatenate(halves(whole), 0)

    made["across_full"] = across(g)
    c, r = np.meshgrid(np.arange(8), np.arange(16), indexing="ij")
    made["across_object"] = across((8 * r + c).reshape(-1))
    cosine, sine = turn(np.arange(256)[:, None] * block_of(g)[None, :], 256)
    made["back_x"] = np.concatenate(halves(np.block([[cosine, -sine], [sine, cosine]])), 0)

    choose = np.zeros((3, 384, 512))
    for kind in range(3):
        for row in range(128):
            slot, v = spectral_s[row], spectral_v[row]

            def own(number):
                return (number // 8) * 64 + v * 8 + number % 8

            def got(number):
                return 256 + (number // 8) * 64 + v * 8 + number % 8

            extra = 384 + v
            if kind == 2:
                plus, minus = got(slot), own(16 - slot)
            else:
                plus, minus = own(slot), (extra if slot == 0 else got(16 - slot))
            if kind == 0 and slot == 0:
                choose[kind, row, plus] = 1.0
                choose[kind, 128 + row, minus] = 1.0
            else:
                for part, sign in ((0, 1.0), (128, 1.0), (256, -1.0)):
                    choose[kind, part + row, plus] = 1.0
                    choose[kind, part + row, minus] = sign
    made["choose"] = choose.astype(ml_dtypes.bfloat16)
    return made


def product(left, right):
    return lax.dot_general(left, right, (((1,), (0,)), ((), ())), preferred_element_type=F32)


def product_turned(left, right):
    return lax.dot_general(left, right, (((1,), (1,)), ((), ())), preferred_element_type=F32)


def split(values):
    high = values.astype(BF16)
    return high, (values - high.astype(F32)).astype(BF16)


def table_first(table, high, low, dot):
    rows = table.shape[0] // 2
    both = dot(table, high)
    return both[:rows] + (both[rows:] + dot(table[:rows], low))


def table_last(values, table):
    depth = table.shape[0] // 2
    rows = values.shape[0]
    high, low = split(values)
    both = product(jnp.concatenate([high, low], 0), table[:depth])
    return both[:rows] + (both[rows:] + product(high, table[depth:]))


def rows_to_half(field, tab, across):
    opened = table_first(tab["open_x"][...], *split(field), product)
    real, imaginary = opened[:128], opened[128:]
    cosine, sine = tab["twist_out"][:128, :], tab["twist_out"][128:, :]
    turned = jnp.concatenate(
        [real * cosine + imaginary * sine, imaginary * cosine - real * sine], 1
    )
    out = table_first(tab[across][...], *split(turned), product_turned)
    row = lax.broadcasted_iota(jnp.int32, (128, 128), 0)
    lane = lax.broadcasted_iota(jnp.int32, (128, 128), 1)
    extra = jnp.where((row == 0) & (lane < 8), out[256:257], 0.0)
    return out[:128], out[128:256] + extra


def half_to_rows(planes, tab):
    back = table_first(tab["back_x"][...], *split(planes), product)
    lane = lax.broadcasted_iota(jnp.int32, (256, 128), 1)
    number = lax.broadcasted_iota(jnp.int32, (256, 128), 0)
    shared = jnp.where(lane < 8, planes[128:129], 0.0)
    real = back[:256] + jnp.where(number % 2 == 0, shared, -shared)
    imaginary = back[256:]
    cosine, sine = tab["twist_in"][:256, :], tab["twist_in"][256:, :]
    turned = jnp.concatenate(
        [real * cosine - imaginary * sine, real * sine + imaginary * cosine], 1
    )
    return table_first(tab["close_x"][...], *split(turned), product_turned)


def spectral_chunk(table, high, low, cosine, sine, tab, weights, conjugate):
    opened = table_first(table, high, low, product)
    real, imaginary = opened[:128], opened[128:]
    cosine2 = jnp.concatenate([cosine, cosine], 1)
    sine2 = jnp.concatenate([sine, sine], 1)
    turned_real = real * cosine2 + imaginary * sine2
    turned_imaginary = imaginary * cosine2 - real * sine2
    stacked = jnp.concatenate(
        [
            jnp.concatenate([turned_real[:, :128], turned_imaginary[:, :128]], 1),
            jnp.concatenate([turned_real[:, 128:], turned_imaginary[:, 128:]], 1),
        ],
        0,
    )
    mixed = table_last(stacked, tab["mix_down"][...])
    ar, ai = mixed[:128, :128], mixed[:128, 128:]
    br, bi = mixed[128:, :128], mixed[128:, 128:]
    (s1r, s1i), (s2r, s2i), (dr, di) = weights
    if conjugate:
        s1i, s2i, di = -s1i, -s2i, -di
    ur = s1r * ar - s1i * ai - (dr * bi + di * br)
    ui = s1r * ai + s1i * ar + (dr * br - di * bi)
    vr = dr * ar - di * ai - (s2r * bi + s2i * br)
    vi = dr * ai + di * ar + (s2r * br - s2i * bi)
    stacked = jnp.concatenate(
        [jnp.concatenate([ur, ui], 1), jnp.concatenate([vr, vi], 1)], 0
    )
    mixed = table_last(stacked, tab["mix_up"][...])
    cosine = jnp.concatenate([cosine, cosine], 0)
    sine = jnp.concatenate([sine, sine], 0)
    real, imaginary = mixed[:, :128], mixed[:, 128:]
    return real * cosine - imaginary * sine, real * sine + imaginary * cosine


NAMES = (
    "open_x",
    "twist_out",
    "across_object",
    "down_object",
    "twist_vertical",
    "mix_down",
    "choose",
    "mix_up",
    "up_full",
    "back_x",
    "twist_in",
    "close_x",
    "across_full",
    "down_full",
    "up_gradient",
)


def kernel(*refs):
    object_ref, images_ref, real_ref, imaginary_ref = refs[:4]
    sources = refs[4 : 4 + len(NAMES)]
    out_ref = refs[4 + len(NAMES)]
    rest = refs[5 + len(NAMES) :]
    tab = dict(zip(NAMES, rest[: len(NAMES)]))
    (
        transfer,
        partner,
        extra_send,
        extra,
        object_rows,
        image_rows,
        send_a,
        got_a,
        send_b,
        pencils,
        weight,
        split_high,
        split_low,
        back_high,
        back_low,
        send_four,
        got_four,
        send_five,
        got_five,
        send_six,
        got_six,
        send_c,
        got_c,
        send_d,
        got_d,
        send_out,
        got_out,
        table_sem,
        local_sem,
        send_sem,
        recv_sem,
    ) = rest[len(NAMES) :]

    frame, row, col = lax.axis_index("frame"), lax.axis_index("row"), lax.axis_index("col")
    me = row * 8 + col

    loads = {
        name: pltpu.make_async_copy(source, tab[name], table_sem.at[number])
        for number, (name, source) in enumerate(zip(NAMES, sources))
    }

    def need(*names):
        for name in names:
            loads[name].wait()

    transfer_loads = [
        pltpu.make_async_copy(real_ref, transfer.at[0], local_sem.at[0]),
        pltpu.make_async_copy(imaginary_ref, transfer.at[1], local_sem.at[1]),
    ]
    object_load = pltpu.make_async_copy(
        object_ref.at[8 * frame + col], object_rows.at[col], local_sem.at[2]
    )
    images_load = pltpu.make_async_copy(
        images_ref.at[pl.ds(4 * col, 4)], image_rows.at[col], local_sem.at[3]
    )
    for load in transfer_loads:
        load.start()
    object_load.start()
    images_load.start()
    for name in NAMES:
        loads[name].start()

    barrier = pltpu.get_barrier_semaphore()

    def greet(step, carry):
        other = lax.rem(me + step, DEVICES)
        pl.semaphore_signal(
            barrier, inc=1, device_id=(frame, other // 8, lax.rem(other, 8)), device_id_type=MESH
        )
        return carry

    lax.fori_loop(1, DEVICES, greet, 0)
    for step in range(1, 4):
        pl.semaphore_signal(
            barrier, inc=1, device_id=(lax.rem(frame + step, 4), row, col), device_id_type=MESH
        )
    pl.semaphore_wait(barrier, DEVICES - 1 + 3)

    def send(source, target, phase, device):
        pltpu.make_async_remote_copy(
            src_ref=source,
            dst_ref=target,
            send_sem=send_sem.at[phase],
            recv_sem=recv_sem.at[phase],
            device_id=device,
            device_id_type=MESH,
        ).start()

    def wait_bytes(like, semaphore):
        pltpu.make_async_copy(like, like, semaphore).wait()

    def each_col(body):
        def step(number, carry):
            body(lax.rem(col + number, 8))
            return carry

        lax.fori_loop(1, 8, step, 0)

    def each_row(body):
        def step(number, carry):
            body(lax.rem(row + number, 16))
            return carry

        lax.fori_loop(1, 16, step, 0)

    def each_frame(body):
        for number in range(1, 4):
            body(lax.rem(frame + number, 4))

    def tile(number):
        return pl.ds(pl.multiple_of(number * 8, 8), 8)

    each_col(
        lambda c: send(
            object_ref.at[8 * frame + c], object_rows.at[col], 0, (frame, row, c)
        )
    )
    for load in transfer_loads:
        load.wait()
    for plane in range(2):
        extra_send[plane] = transfer[plane, 0, pl.ds(0, 32, stride=8), :]
    opposite = 127 - me
    is_end = 1 - (lax.rem(me, 64) + 63) // 64
    beyond = 128 - me - 64 * is_end
    send(extra_send, extra, 2, (frame, beyond // 8, lax.rem(beyond, 8)))
    for plane in range(2):
        send(
            transfer.at[plane, pl.ds(2, 2)],
            partner.at[plane],
            3 + plane,
            (frame, opposite // 8, lax.rem(opposite, 8)),
        )
    each_col(
        lambda c: send(
            images_ref.at[pl.ds(4 * c, 4)], image_rows.at[col], 1, (frame, row, c)
        )
    )

    def field_of(read):
        return jnp.concatenate(
            [
                jnp.concatenate([read(x1 // 2, 2 * (x1 % 2) + part) for x1 in range(16)], 0)
                for part in range(2)
            ],
            1,
        )

    object_load.wait()
    wait_bytes(object_rows.at[pl.ds(0, 7)], recv_sem.at[0])
    need("open_x", "twist_out", "across_object")
    planes = rows_to_half(field_of(lambda c, k: object_rows[c, k]), tab, "across_object")
    for plane in range(2):
        for c in range(8):
            send_a[c, plane] = planes[plane][16 * c : 16 * c + 16]
    got_a[pl.ds(pl.multiple_of(col * 32, 32), 32), :] = send_a[col].reshape(32, 128)
    each_col(
        lambda c: send(
            send_a.at[c].reshape(32, 128),
            got_a.at[pl.ds(pl.multiple_of(col * 32, 32), 32)],
            5,
            (frame, row, c),
        )
    )

    def cross_rows(got, sends, phase, target):
        wait_bytes(got.at[pl.ds(0, 7 * 32)], recv_sem.at[phase])
        for r in range(16):
            sends[r] = got[pl.ds(r, 16, stride=16), :]
        target[row] = sends[row]
        each_row(lambda r: send(sends.at[r], target.at[row], phase + 1, (frame, r, col)))
        wait_bytes(sends.at[pl.ds(0, 15)], recv_sem.at[phase + 1])

    def quarter(number):
        return pencils.at[pl.ds(pl.multiple_of(number * 16, 16), 16)]

    cross_rows(got_a, send_b, 5, quarter(frame))
    each_frame(lambda f: send(quarter(frame), quarter(frame), 7, (f, row, col)))
    wait_bytes(pencils.at[pl.ds(0, 48)], recv_sem.at[7])

    wait_bytes(extra, recv_sem.at[2])
    for plane in range(2):
        wait_bytes(partner.at[plane], recv_sem.at[3 + plane])
    need("choose")
    kind = (me + 127) // 128 + me // 64
    for part in range(4):
        blocks = []
        for plane in range(2):
            rows = [
                transfer[plane, a, pl.ds((4 * v + part) * 8, 8), :]
                for a in range(4)
                for v in range(8)
            ]
            rows += [
                partner[plane, a, pl.ds((4 * v + part) * 8, 8), :]
                for a in range(2)
                for v in range(8)
            ]
            rows += [extra[plane, pl.ds(part, 8, stride=4), :], jnp.zeros((120, 128), F32)]
            blocks.append(jnp.concatenate(rows, 0))
        block = jnp.concatenate(blocks, 1)
        first = block.astype(BF16)
        left = block - first.astype(F32)
        second = left.astype(BF16)
        third = (left - second.astype(F32)).astype(BF16)
        chosen = tab["choose"][kind]
        picked = product(chosen, first) + (product(chosen, second) + product(chosen, third))
        for number in range(3):
            for plane in range(2):
                weight[number, plane, pl.ds(128 * part, 128), :] = picked[
                    128 * number : 128 * number + 128, 128 * plane : 128 * plane + 128
                ].T

    def through(down, conjugate):
        def chunk(number, carry):
            rows = pl.ds(pl.multiple_of(number * 128, 128), 128)
            weights = [(weight[k, 0, rows, :], weight[k, 1, rows, :]) for k in range(3)]
            real, imaginary = spectral_chunk(
                tab[down][pl.ds(pl.multiple_of(number * 512, 512), 512), :],
                split_high[...],
                split_low[...],
                tab["twist_vertical"][rows, :],
                tab["twist_vertical"][pl.ds(pl.multiple_of(512 + number * 128, 128), 128), :],
                tab,
                weights,
                conjugate,
            )
            for plane, values in enumerate((real, imaginary)):
                high, low = split(values)
                for which in range(2):
                    part = slice(128 * which, 128 * which + 128)
                    at = pl.ds(pl.multiple_of(512 * plane + number * 128, 128), 128)
                    back_high[which, at, :] = high[part]
                    back_low[which, at, :] = low[part]
            return carry

        lax.fori_loop(0, 4, chunk, 0)

    def return_chunk(up, number):
        table = tab[up][pl.ds(pl.multiple_of(number * 256, 256), 256), :]
        real = table_first(table[:, 512:], back_high[0], back_low[0], product)
        imaginary = table_first(table[:, :1024], back_high[1], back_low[1], product)
        return real, imaginary

    def to_all(source, target, phase):
        target[tile(me), :] = source[tile(me), :]

        def step(number, carry):
            other = lax.rem(me + number, DEVICES)
            send(
                source.at[tile(other)],
                target.at[tile(me)],
                phase,
                (frame, other // 8, lax.rem(other, 8)),
            )
            return carry

        lax.fori_loop(1, DEVICES, step, 0)

    for plane in range(2):
        high, low = split(
            pencils.reshape(1024, 128)[pl.ds(plane, 512, stride=2), :]
        )
        split_high[:, 128 * plane : 128 * plane + 128] = high
        split_low[:, 128 * plane : 128 * plane + 128] = low
    need("down_object", "twist_vertical", "mix_down", "mix_up")
    through("down_object", False)
    need("up_full")
    for number in range(4):
        real, imaginary = return_chunk("up_full", number)
        send_four[pl.ds(number, 128, stride=8), :] = real
        send_four[pl.ds(4 + number, 128, stride=8), :] = imaginary
    to_all(send_four, got_four, 8)

    images_load.wait()
    wait_bytes(image_rows.at[pl.ds(0, 7)], recv_sem.at[1])
    need("back_x", "twist_in", "close_x", "across_full")
    wait_bytes(got_four.at[pl.ds(0, 127 * 8)], recv_sem.at[8])
    for number in range(4):
        modelled = half_to_rows(
            jnp.concatenate(
                [
                    got_four[pl.ds(number, 128, stride=8), :],
                    got_four[pl.ds(4 + number, 128, stride=8), :],
                ],
                0,
            ),
            tab,
        )
        images = field_of(lambda c, k: image_rows[c, number, k])
        weighted = (modelled - images) / (0.5 + jnp.abs(images))
        planes = rows_to_half(weighted, tab, "across_full")
        for plane in range(2):
            send_five[pl.ds(4 * plane + number, 128, stride=8), :] = planes[plane]
    to_all(send_five, got_five, 9)

    need("down_full", "up_gradient")
    wait_bytes(got_five.at[pl.ds(0, 127 * 8)], recv_sem.at[9])
    for plane in range(2):
        for number in range(4):
            high, low = split(got_five[pl.ds(4 * plane + number, 128, stride=8), :])
            at = (slice(128 * number, 128 * number + 128), slice(128 * plane, 128 * plane + 128))
            split_high[at] = high
            split_low[at] = low
    through("down_full", True)
    for number in range(4):
        planes = return_chunk("up_gradient", number)
        for plane in range(2):
            for c in range(8):
                send_six[number, c, plane] = planes[plane][16 * c : 16 * c + 16]

    each_frame(lambda f: send(send_six.at[f], got_six.at[frame], 10, (f, row, col)))
    got_six[frame] = send_six[frame]
    wait_bytes(send_six.at[pl.ds(0, 3)], recv_sem.at[10])
    send_c[...] = (got_six[0] + got_six[1]) + (got_six[2] + got_six[3])
    got_c[pl.ds(pl.multiple_of(col * 32, 32), 32), :] = send_c[col].reshape(32, 128)
    each_col(
        lambda c: send(
            send_c.at[c].reshape(32, 128),
            got_c.at[pl.ds(pl.multiple_of(col * 32, 32), 32)],
            11,
            (frame, row, c),
        )
    )
    cross_rows(got_c, send_d, 11, got_d)
    flat = got_d.reshape(256, 128)
    field = half_to_rows(
        jnp.concatenate([flat[pl.ds(0, 128, stride=2), :], flat[pl.ds(1, 128, stride=2), :]], 0),
        tab,
    )
    for x1 in range(16):
        for part in range(2):
            send_out[x1 // 2, 2 * (x1 % 2) + part] = field[
                8 * x1 : 8 * x1 + 8, 128 * part : 128 * part + 128
            ]
    got_out[col] = send_out[col]
    each_col(lambda c: send(send_out.at[c], got_out.at[col], 13, (frame, row, c)))
    wait_bytes(send_out.at[pl.ds(0, 7)], recv_sem.at[13])
    out_ref[...] = got_out[...]

    wait_bytes(object_rows.at[pl.ds(0, 7)], send_sem.at[0])
    wait_bytes(image_rows.at[pl.ds(0, 7)], send_sem.at[1])
    wait_bytes(extra, send_sem.at[2])
    for plane in range(2):
        wait_bytes(partner.at[plane], send_sem.at[3 + plane])
    wait_bytes(got_a.at[pl.ds(0, 7 * 32)], send_sem.at[5])
    wait_bytes(send_b.at[pl.ds(0, 15)], send_sem.at[6])
    wait_bytes(pencils.at[pl.ds(0, 48)], send_sem.at[7])
    wait_bytes(got_four.at[pl.ds(0, 127 * 8)], send_sem.at[8])
    wait_bytes(got_five.at[pl.ds(0, 127 * 8)], send_sem.at[9])
    wait_bytes(send_six.at[pl.ds(0, 3)], send_sem.at[10])
    wait_bytes(got_c.at[pl.ds(0, 7 * 32)], send_sem.at[11])
    wait_bytes(send_d.at[pl.ds(0, 15)], send_sem.at[12])
    wait_bytes(send_out.at[pl.ds(0, 7)], send_sem.at[13])


def tiles(block):
    rows, columns = block.shape
    return block.reshape(rows // 8, 8, columns // 128, 128).transpose(0, 2, 1, 3)


def shards(object_field, images, transfer_real, transfer_imaginary):
    made = tables()
    operands = [made[name] for name in NAMES]
    scratch = [pltpu.VMEM(table.shape, table.dtype) for table in operands]
    scratch += [
        pltpu.VMEM((2, 4, 256, 128), F32),
        pltpu.VMEM((2, 2, 256, 128), F32),
        pltpu.VMEM((2, 32, 128), F32),
        pltpu.VMEM((2, 32, 128), F32),
        pltpu.VMEM((8, 4, 8, 128), F32),
        pltpu.VMEM((8, 4, 4, 8, 128), F32),
        pltpu.VMEM((8, 2, 16, 128), F32),
        pltpu.VMEM((256, 128), F32),
        pltpu.VMEM((16, 16, 128), F32),
        pltpu.VMEM((64, 16, 128), F32),
        pltpu.VMEM((3, 2, 512, 128), F32),
        pltpu.VMEM((512, 256), BF16),
        pltpu.VMEM((512, 256), BF16),
        pltpu.VMEM((2, 1024, 128), BF16),
        pltpu.VMEM((2, 1024, 128), BF16),
        pltpu.VMEM((1024, 128), F32),
        pltpu.VMEM((1024, 128), F32),
        pltpu.VMEM((1024, 128), F32),
        pltpu.VMEM((1024, 128), F32),
        pltpu.VMEM((4, 8, 2, 16, 128), F32),
        pltpu.VMEM((4, 8, 2, 16, 128), F32),
        pltpu.VMEM((8, 2, 16, 128), F32),
        pltpu.VMEM((256, 128), F32),
        pltpu.VMEM((16, 16, 128), F32),
        pltpu.VMEM((16, 16, 128), F32),
        pltpu.VMEM((8, 4, 8, 128), F32),
        pltpu.VMEM((8, 4, 8, 128), F32),
        pltpu.SemaphoreType.DMA((len(NAMES),)),
        pltpu.SemaphoreType.DMA((4,)),
        pltpu.SemaphoreType.DMA((14,)),
        pltpu.SemaphoreType.DMA((14,)),
    ]
    anywhere = pl.BlockSpec(memory_space=pl.ANY)
    block = pl.pallas_call(
        kernel,
        out_shape=jax.ShapeDtypeStruct((8, 4, 8, 128), F32),
        in_specs=[anywhere] * (4 + len(NAMES)),
        out_specs=pl.BlockSpec(memory_space=pltpu.VMEM),
        scratch_shapes=scratch,
        compiler_params=pltpu.CompilerParams(
            collective_id=0, has_side_effects=True, vmem_limit_bytes=56 * 1024 * 1024
        ),
        name="gradient",
    )(
        tiles(object_field),
        tiles(images[0]),
        tiles(transfer_real[0]).reshape(4, 256, 128),
        tiles(transfer_imaginary[0]).reshape(4, 256, 128),
        *operands,
    )
    return block.transpose(0, 2, 1, 3).reshape(64, 512)


def solution(mesh):
    placed = (
        P("row", "col"),
        P("frame", "row", "col"),
        P("frame", ("row", "col"), None),
        P("frame", ("row", "col"), None),
    )
    return jax.shard_map(
        shards, mesh=mesh, in_specs=placed, out_specs=P(("frame", "row"), "col"), check_vma=False
    )
```

```python
import functools
import math

import jax
import jax.numpy as jnp
import ml_dtypes
import numpy as np
from jax import lax
from jax.experimental import pallas as pl
from jax.experimental.pallas import tpu as pltpu
from jax.sharding import PartitionSpec as P

F32 = jnp.float32
BF16 = jnp.bfloat16
MESH = pl.DeviceIdType.MESH

N = 4096
DEVICES = 128


def block_of(g):
    return np.where(g < 64, 2 * g, 2 * (127 - g) + 1)


def halves(table):
    high = table.astype(np.float32).astype(ml_dtypes.bfloat16)
    low = (table - high.astype(np.float64)).astype(np.float32).astype(ml_dtypes.bfloat16)
    return high, low


def turn(numbers, length):
    angles = 2.0 * math.pi / length * (numbers % length)
    return np.cos(angles), np.sin(angles)


def vertical_forward(order):
    cosine, sine = turn(np.arange(512)[:, None] * order[None, :], 512)
    pieces = []
    for chunk in range(4):
        rows = slice(128 * chunk, 128 * chunk + 128)
        high, low = halves(np.concatenate([cosine[rows], -sine[rows]], 0))
        pieces += [high, low]
    return np.concatenate(pieces, 0)


def vertical_inverse(order):
    cosine, sine = turn(order[:, None] * np.arange(512)[None, :], 512)
    whole = np.concatenate([sine, cosine, -sine], 1)
    pieces = []
    for chunk in range(4):
        pieces += list(halves(whole[128 * chunk : 128 * chunk + 128]))
    return np.concatenate(pieces, 0)


def tables():
    made = {}
    g = np.arange(128)
    full = (4 * g[None, :] + np.arange(4)[:, None]).reshape(-1)
    f, r, c = np.meshgrid(np.arange(4), np.arange(16), np.arange(8), indexing="ij")
    made["down_object"] = vertical_forward((32 * r + 8 * f + c).reshape(-1))
    made["down_full"] = vertical_forward(full)
    made["up_full"] = vertical_inverse(full)
    made["up_gradient"] = vertical_inverse(np.arange(512))

    s, t = np.meshgrid(np.arange(16), np.arange(8), indexing="ij")
    s, t = s.reshape(-1), t.reshape(-1)
    sh, v1, sl = np.meshgrid(np.arange(2), np.arange(8), np.arange(8), indexing="ij")
    spectral_s, spectral_v = (8 * sh + sl).reshape(-1), v1.reshape(-1)
    cosine, sine = turn(t[:, None] * spectral_v[None, :], 8)
    same = (s[:, None] == spectral_s[None, :]).astype(np.float64)
    cosine, sine = cosine * same, sine * same
    made["mix_down"] = np.concatenate(halves(np.block([[cosine, -sine], [sine, cosine]])), 0)
    made["mix_up"] = np.concatenate(halves(np.block([[cosine.T, sine.T], [-sine.T, cosine.T]])), 0)
    cosine, sine = turn(np.arange(512)[:, None] * t[None, :], 4096)
    made["twist_vertical"] = np.concatenate([cosine, sine], 0).astype(np.float32)

    x1, tx = s, t
    same = (t[:, None] == tx[None, :]).astype(np.float64)
    cosine, sine = turn(s[:, None] * x1[None, :], 16)
    cosine, sine = cosine * same, sine * same
    made["open_x"] = np.concatenate(halves(np.concatenate([cosine, -sine], 0)), 0)
    scale = 1.0 / (float(N) * float(N))
    made["close_x"] = np.concatenate(halves(np.concatenate([cosine.T, -sine.T], 1) * scale), 0)
    cosine, sine = turn(s[:, None] * np.arange(256)[None, :], 4096)
    made["twist_out"] = np.concatenate([cosine, sine], 0).astype(np.float32)
    made["twist_in"] = np.concatenate([cosine.T, sine.T], 0).astype(np.float32)

    cosine, sine = turn(block_of(g)[:, None] * np.arange(256)[None, :], 256)
    alternate = np.zeros((16, 512))
    alternate[0, :256] = 1.0 - 2.0 * (np.arange(256) % 2)
    whole = np.block([[cosine, sine], [-sine, cosine]])
    made["across"] = np.concatenate(halves(np.concatenate([whole, alternate], 0)), 0)
    cosine, sine = turn(np.arange(256)[:, None] * block_of(g)[None, :], 256)
    made["back_x"] = np.concatenate(halves(np.block([[cosine, -sine], [sine, cosine]])), 0)

    choose = np.zeros((3, 384, 512))
    for kind in range(3):
        for row in range(128):
            slot, v = spectral_s[row], spectral_v[row]

            def own(number):
                return (number // 8) * 64 + v * 8 + number % 8

            def got(number):
                return 256 + (number // 8) * 64 + v * 8 + number % 8

            extra = 384 + v
            if kind == 2:
                plus, minus = got(slot), own(16 - slot)
            else:
                plus, minus = own(slot), (extra if slot == 0 else got(16 - slot))
            if kind == 0 and slot == 0:
                choose[kind, row, plus] = 1.0
                choose[kind, 128 + row, minus] = 1.0
            else:
                for part, sign in ((0, 1.0), (128, 1.0), (256, -1.0)):
                    choose[kind, part + row, plus] = 1.0
                    choose[kind, part + row, minus] = sign
    made["choose"] = choose.astype(ml_dtypes.bfloat16)
    return made


def product(left, right):
    return lax.dot_general(left, right, (((1,), (0,)), ((), ())), preferred_element_type=F32)


def product_turned(left, right):
    return lax.dot_general(left, right, (((1,), (1,)), ((), ())), preferred_element_type=F32)


def split(values):
    high = values.astype(BF16)
    return high, (values - high.astype(F32)).astype(BF16)


def table_first(table, high, low, dot):
    rows = table.shape[0] // 2
    both = dot(table, high)
    return both[:rows] + (both[rows:] + dot(table[:rows], low))


def table_last(values, table):
    depth = table.shape[0] // 2
    rows = values.shape[0]
    high, low = split(values)
    both = product(jnp.concatenate([high, low], 0), table[:depth])
    return both[:rows] + (both[rows:] + product(high, table[depth:]))


def rows_to_half(fields, tab):
    opened = table_first(tab["open_x"][...], *split(jnp.concatenate(fields, 1)), product)
    cosine, sine = tab["twist_out"][:128, :], tab["twist_out"][128:, :]
    turned = []
    for number in range(len(fields)):
        part = slice(256 * number, 256 * number + 256)
        real, imaginary = opened[:128, part], opened[128:, part]
        turned.append(
            jnp.concatenate(
                [real * cosine + imaginary * sine, imaginary * cosine - real * sine], 1
            )
        )
    out = table_first(tab["across"][...], *split(jnp.concatenate(turned, 0)), product_turned)
    row = lax.broadcasted_iota(jnp.int32, (128, 128), 0)
    lane = lax.broadcasted_iota(jnp.int32, (128, 128), 1)
    shared = (row == 0) & (lane < 8)
    pairs = []
    for number in range(len(fields)):
        part = slice(128 * number, 128 * number + 128)
        extra = jnp.where(shared, out[256:257, part], 0.0)
        pairs.append((out[:128, part], out[128:256, part] + extra))
    return pairs


def half_to_rows(planes, tab):
    back = table_first(tab["back_x"][...], *split(jnp.concatenate(planes, 1)), product)
    lane = lax.broadcasted_iota(jnp.int32, (256, 128), 1)
    number = lax.broadcasted_iota(jnp.int32, (256, 128), 0)
    cosine, sine = tab["twist_in"][:256, :], tab["twist_in"][256:, :]
    fields = []
    for which, plane in enumerate(planes):
        part = slice(128 * which, 128 * which + 128)
        shared = jnp.where(lane < 8, plane[128:129], 0.0)
        real = back[:256, part] + jnp.where(number % 2 == 0, shared, -shared)
        imaginary = back[256:, part]
        turned = jnp.concatenate(
            [real * cosine - imaginary * sine, real * sine + imaginary * cosine], 1
        )
        fields.append(table_first(tab["close_x"][...], *split(turned), product_turned))
    return fields


def down_chunk(table, high, low, cosine, sine, tab):
    opened = table_first(table, high, low, product)
    real, imaginary = opened[:128], opened[128:]
    cosine = jnp.concatenate([cosine, cosine], 1)
    sine = jnp.concatenate([sine, sine], 1)
    turned_real = real * cosine + imaginary * sine
    turned_imaginary = imaginary * cosine - real * sine
    stacked = jnp.concatenate(
        [
            jnp.concatenate([turned_real[:, :128], turned_imaginary[:, :128]], 1),
            jnp.concatenate([turned_real[:, 128:], turned_imaginary[:, 128:]], 1),
        ],
        0,
    )
    return table_last(stacked, tab["mix_down"][...])


def up_chunk(mixed, cosine, sine, tab, weights, conjugate):
    ar, ai = mixed[:128, :128], mixed[:128, 128:]
    br, bi = mixed[128:, :128], mixed[128:, 128:]
    (s1r, s1i), (s2r, s2i), (dr, di) = weights
    if conjugate:
        s1i, s2i, di = -s1i, -s2i, -di
    ur = s1r * ar - s1i * ai - (dr * bi + di * br)
    ui = s1r * ai + s1i * ar + (dr * br - di * bi)
    vr = dr * ar - di * ai - (s2r * bi + s2i * br)
    vi = dr * ai + di * ar + (s2r * br - s2i * bi)
    stacked = jnp.concatenate(
        [jnp.concatenate([ur, ui], 1), jnp.concatenate([vr, vi], 1)], 0
    )
    mixed = table_last(stacked, tab["mix_up"][...])
    cosine = jnp.concatenate([cosine, cosine], 0)
    sine = jnp.concatenate([sine, sine], 0)
    real, imaginary = mixed[:, :128], mixed[:, 128:]
    return real * cosine - imaginary * sine, real * sine + imaginary * cosine


NAMES = (
    "open_x",
    "twist_out",
    "across",
    "down_object",
    "twist_vertical",
    "mix_down",
    "choose",
    "mix_up",
    "up_full",
    "back_x",
    "twist_in",
    "close_x",
    "down_full",
    "up_gradient",
)


def kernel(*refs):
    object_ref, images_ref, real_ref, imaginary_ref = refs[:4]
    sources = refs[4 : 4 + len(NAMES)]
    out_ref = refs[4 + len(NAMES)]
    rest = refs[5 + len(NAMES) :]
    tab = dict(zip(NAMES, rest[: len(NAMES)]))
    (
        transfer,
        partner,
        extra_send,
        extra,
        object_rows,
        image_rows,
        send_a,
        pencils,
        middle,
        weight,
        split_high,
        split_low,
        back_high,
        back_low,
        send_four,
        got_four,
        send_five,
        got_five,
        send_six,
        got_six,
        send_c,
        got_d,
        send_out,
        got_out,
        table_sem,
        local_sem,
        send_sem,
        recv_sem,
    ) = rest[len(NAMES) :]

    frame, row, col = lax.axis_index("frame"), lax.axis_index("row"), lax.axis_index("col")
    me = row * 8 + col

    loads = {
        name: pltpu.make_async_copy(source, tab[name], table_sem.at[number])
        for number, (name, source) in enumerate(zip(NAMES, sources))
    }

    def need(*names):
        for name in names:
            loads[name].wait()

    transfer_loads = [
        pltpu.make_async_copy(real_ref, transfer.at[0], local_sem.at[0]),
        pltpu.make_async_copy(imaginary_ref, transfer.at[1], local_sem.at[1]),
    ]
    object_load = pltpu.make_async_copy(
        object_ref.at[8 * frame + col], object_rows.at[col], local_sem.at[2]
    )
    images_load = pltpu.make_async_copy(
        images_ref.at[pl.ds(4 * col, 4)], image_rows.at[col], local_sem.at[3]
    )
    for load in transfer_loads:
        load.start()
    object_load.start()
    images_load.start()
    for name in NAMES:
        loads[name].start()

    barrier = pltpu.get_barrier_semaphore()

    columns = [lax.rem(col + number, 8) for number in range(8)]

    def each_peer(body):
        for c in columns[1:]:
            body(row, c)

        def step(number, carry):
            r = lax.rem(row + number, 16)
            for c in columns:
                body(r, c)
            return carry

        lax.fori_loop(1, 16, step, 0)

    opposite = 127 - me
    is_end = 1 - (lax.rem(me, 64) + 63) // 64
    beyond = 128 - me - 64 * is_end
    mirror = (frame, opposite // 8, lax.rem(opposite, 8))
    after = (frame, beyond // 8, lax.rem(beyond, 8))

    def greet(device):
        pl.semaphore_signal(barrier, inc=1, device_id=device, device_id_type=MESH)

    greet(mirror)
    greet(after)
    for c in columns[1:]:
        greet((frame, row, c))

    def greet_row(number, carry):
        greet((frame, lax.rem(row + number, 16), col))
        return carry

    lax.fori_loop(1, 16, greet_row, 0)
    for step in range(1, 4):
        greet((lax.rem(frame + step, 4), row, col))
    pl.semaphore_wait(barrier, 2 + 7 + 15 + 3)

    def send(source, target, phase, device):
        pltpu.make_async_remote_copy(
            src_ref=source,
            dst_ref=target,
            send_sem=send_sem.at[phase],
            recv_sem=recv_sem.at[phase],
            device_id=device,
            device_id_type=MESH,
        ).start()

    def wait_bytes(like, semaphore):
        pltpu.make_async_copy(like, like, semaphore).wait()

    def each_col(body):
        for c in columns[1:]:
            body(c)

    def each_frame(body):
        for number in range(1, 4):
            body(lax.rem(frame + number, 4))

    def block(number, size):
        return pl.ds(pl.multiple_of(number * size, size), size)

    each_col(
        lambda c: send(
            object_ref.at[8 * frame + c], object_rows.at[col], 0, (frame, row, c)
        )
    )
    for load in transfer_loads:
        load.wait()
    for plane in range(2):
        extra_send[plane] = transfer[plane, 0, pl.ds(0, 32, stride=8), :]
    def send_partner(number):
        plane, a, part = number // 8, lax.rem(number // 4, 2), lax.rem(number, 4)
        rows = block(part, 64)
        send(transfer.at[plane, 2 + a, rows], partner.at[plane, a, rows], 3, mirror)

    def send_image(c):
        send(images_ref.at[pl.ds(4 * c, 4)], image_rows.at[col], 1, (frame, row, c))

    for number in range(3):
        send_partner(number)

    def field_of(read):
        return jnp.concatenate(
            [
                jnp.concatenate([read(x1 // 2, 2 * (x1 % 2) + part) for x1 in range(16)], 0)
                for part in range(2)
            ],
            1,
        )

    def to_all(source, target, size, phase):
        target[block(me, size), :] = source[block(me, size), :]
        own = block(me, size)
        each_peer(
            lambda r, c: send(
                source.at[block(r * 8 + c, size)], target.at[own], phase, (frame, r, c)
            )
        )

    object_load.wait()
    wait_bytes(object_rows.at[pl.ds(0, 7)], recv_sem.at[0])
    need("open_x", "twist_out", "across")
    planes = rows_to_half([field_of(lambda c, k: object_rows[c, k])], tab)[0]
    for plane in range(2):
        send_a[pl.ds(plane, 128, stride=2), :] = planes[plane]
    quarter = pencils.at[block(frame, 256)]
    quarter[block(me, 2), :] = send_a[block(me, 2), :]

    def send_pencil(r, c):
        send(send_a.at[block(r * 8 + c, 2)], quarter.at[block(me, 2)], 5, (frame, r, c))

    for c in columns[1:]:
        send_pencil(row, c)

    def some_rows(step, carry):
        for number in range(1, 6):
            for c in columns:
                send_pencil(lax.rem(row + 5 * step + number, 16), c)
        send_partner(3 + step)
        return carry

    lax.fori_loop(0, 3, some_rows, 0)
    send(extra_send, extra, 2, after)
    for number in range(6, 16):
        send_partner(number)
        if number >= 9:
            send_image(columns[number - 8])
    wait_bytes(send_a.at[pl.ds(0, 254)], recv_sem.at[5])
    each_frame(lambda f: send(quarter, quarter, 7, (f, row, col)))
    wait_bytes(pencils.at[pl.ds(0, 768)], recv_sem.at[7])

    def turns(number):
        return (
            tab["twist_vertical"][pl.ds(128 * number, 128), :],
            tab["twist_vertical"][pl.ds(512 + 128 * number, 128), :],
        )

    def down(name, number):
        return down_chunk(
            tab[name][pl.ds(512 * number, 512), :],
            split_high[...],
            split_low[...],
            *turns(number),
            tab,
        )

    def up(mixed, number, conjugate):
        rows = pl.ds(128 * number, 128)
        weights = [(weight[k, 0, rows, :], weight[k, 1, rows, :]) for k in range(3)]
        planes = up_chunk(mixed, *turns(number), tab, weights, conjugate)
        for plane, values in enumerate(planes):
            high, low = split(values)
            for which in range(2):
                part = slice(128 * which, 128 * which + 128)
                at = pl.ds(512 * plane + 128 * number, 128)
                back_high[which, at, :] = high[part]
                back_low[which, at, :] = low[part]

    for plane in range(2):
        high, low = split(pencils[pl.ds(plane, 512, stride=2), :])
        split_high[:, 128 * plane : 128 * plane + 128] = high
        split_low[:, 128 * plane : 128 * plane + 128] = low
    need("down_object", "twist_vertical", "mix_down")
    for number in range(4):
        middle[number] = down("down_object", number)

    wait_bytes(extra, recv_sem.at[2])
    wait_bytes(partner, recv_sem.at[3])
    need("choose")
    kind = (me + 127) // 128 + me // 64
    for part in range(4):
        blocks = []
        for plane in range(2):
            rows = [
                transfer[plane, a, pl.ds((4 * v + part) * 8, 8), :]
                for a in range(4)
                for v in range(8)
            ]
            rows += [
                partner[plane, a, pl.ds((4 * v + part) * 8, 8), :]
                for a in range(2)
                for v in range(8)
            ]
            rows += [extra[plane, pl.ds(part, 8, stride=4), :], jnp.zeros((120, 128), F32)]
            blocks.append(jnp.concatenate(rows, 0))
        gathered = jnp.concatenate(blocks, 1)
        first = gathered.astype(BF16)
        left = gathered - first.astype(F32)
        second = left.astype(BF16)
        third = (left - second.astype(F32)).astype(BF16)
        chosen = tab["choose"][kind]
        picked = product(chosen, first) + (product(chosen, second) + product(chosen, third))
        for number in range(3):
            for plane in range(2):
                weight[number, plane, pl.ds(128 * part, 128), :] = picked[
                    128 * number : 128 * number + 128, 128 * plane : 128 * plane + 128
                ].T

    def return_chunk(name, number):
        table = tab[name][block(number, 256), :]
        real = table_first(table[:, 512:], back_high[0], back_low[0], product)
        imaginary = table_first(table[:, :1024], back_high[1], back_low[1], product)
        return real, imaginary

    need("mix_up")
    for number in range(4):
        up(middle[number], number, False)
    need("up_full")
    for number in range(4):
        real, imaginary = return_chunk("up_full", number)
        send_four[pl.ds(number, 128, stride=8), :] = real
        send_four[pl.ds(4 + number, 128, stride=8), :] = imaginary
    to_all(send_four, got_four, 8, 8)

    images_load.wait()
    wait_bytes(image_rows.at[pl.ds(0, 7)], recv_sem.at[1])
    need("back_x", "twist_in", "close_x")
    wait_bytes(got_four.at[pl.ds(0, 127 * 8)], recv_sem.at[8])
    for first in (0, 2):
        both = (first, first + 1)
        modelled = half_to_rows(
            [
                jnp.concatenate(
                    [
                        got_four[pl.ds(number, 128, stride=8), :],
                        got_four[pl.ds(4 + number, 128, stride=8), :],
                    ],
                    0,
                )
                for number in both
            ],
            tab,
        )
        weighted = []
        for number, model in zip(both, modelled):
            images = field_of(lambda c, k: image_rows[c, number, k])
            weighted.append((model - images) / (0.5 + jnp.abs(images)))
        for number, planes in zip(both, rows_to_half(weighted, tab)):
            for plane in range(2):
                send_five[pl.ds(4 * plane + number, 128, stride=8), :] = planes[plane]
    to_all(send_five, got_five, 8, 9)

    need("down_full", "up_gradient")
    wait_bytes(got_five.at[pl.ds(0, 127 * 8)], recv_sem.at[9])
    for plane in range(2):
        for number in range(4):
            high, low = split(got_five[pl.ds(4 * plane + number, 128, stride=8), :])
            at = (slice(128 * number, 128 * number + 128), slice(128 * plane, 128 * plane + 128))
            split_high[at] = high
            split_low[at] = low
    for number in range(4):
        up(down("down_full", number), number, True)

    near = row // 8
    parts = [block(near, 128), block(1 - near, 128)]
    for step in (2, 1, 3, 0):
        f = lax.rem(frame + step, 4)
        planes = return_chunk("up_gradient", f)
        target = got_six if step == 0 else send_six
        for plane in range(2):
            target[f, pl.ds(plane, 128, stride=2), :] = planes[plane]
        if step > 0:
            send(send_six.at[f, parts[0]], got_six.at[frame, parts[0]], 4, (f, row, col))
    for step in (2, 1, 3):
        f = lax.rem(frame + step, 4)
        send(send_six.at[f, parts[1]], got_six.at[frame, parts[1]], 10, (f, row, col))
    for half in range(2):
        wait_bytes(send_six.at[pl.ds(0, 3), pl.ds(0, 128)], recv_sem.at[4 if half == 0 else 10])
        pieces = [got_six[f, parts[half], :] for f in range(4)]
        send_c[parts[half], :] = (pieces[0] + pieces[1]) + (pieces[2] + pieces[3])
        first = 8 * near if half == 0 else 8 - 8 * near

        def send_quarter(r, c):
            send(send_c.at[block(r * 8 + c, 2)], got_d.at[block(me, 2)], 11, (frame, r, c))

        def some_rows(number, carry):
            for c in columns:
                send_quarter(first + lax.rem(row + number, 8), c)
            return carry

        if half == 0:
            got_d[block(me, 2), :] = send_c[block(me, 2), :]
            for c in columns[1:]:
                send_quarter(row, c)
        lax.fori_loop(1 - half, 8, some_rows, 0)
    wait_bytes(send_c.at[pl.ds(0, 254)], recv_sem.at[11])
    field = half_to_rows(
        [jnp.concatenate([got_d[pl.ds(0, 128, stride=2), :], got_d[pl.ds(1, 128, stride=2), :]], 0)],
        tab,
    )[0]
    for x1 in range(16):
        for part in range(2):
            send_out[x1 // 2, 2 * (x1 % 2) + part] = field[
                8 * x1 : 8 * x1 + 8, 128 * part : 128 * part + 128
            ]
    got_out[col] = send_out[col]
    each_col(lambda c: send(send_out.at[c], got_out.at[col], 13, (frame, row, c)))
    wait_bytes(send_out.at[pl.ds(0, 7)], recv_sem.at[13])
    out_ref[...] = got_out[...]

    wait_bytes(object_rows.at[pl.ds(0, 7)], send_sem.at[0])
    wait_bytes(image_rows.at[pl.ds(0, 7)], send_sem.at[1])
    wait_bytes(extra, send_sem.at[2])
    wait_bytes(partner, send_sem.at[3])
    wait_bytes(send_a.at[pl.ds(0, 254)], send_sem.at[5])
    wait_bytes(pencils.at[pl.ds(0, 768)], send_sem.at[7])
    wait_bytes(got_four.at[pl.ds(0, 127 * 8)], send_sem.at[8])
    wait_bytes(got_five.at[pl.ds(0, 127 * 8)], send_sem.at[9])
    wait_bytes(send_six.at[pl.ds(0, 3), pl.ds(0, 128)], send_sem.at[4])
    wait_bytes(send_six.at[pl.ds(0, 3), pl.ds(0, 128)], send_sem.at[10])
    wait_bytes(send_c.at[pl.ds(0, 254)], send_sem.at[11])
    wait_bytes(send_out.at[pl.ds(0, 7)], send_sem.at[13])


def tiles(block):
    rows, columns = block.shape
    return block.reshape(rows // 8, 8, columns // 128, 128).transpose(0, 2, 1, 3)


def shards(object_field, images, transfer_real, transfer_imaginary):
    made = tables()
    operands = [made[name] for name in NAMES]
    scratch = [pltpu.VMEM(table.shape, table.dtype) for table in operands]
    scratch += [
        pltpu.VMEM((2, 4, 256, 128), F32),
        pltpu.VMEM((2, 2, 256, 128), F32),
        pltpu.VMEM((2, 32, 128), F32),
        pltpu.VMEM((2, 32, 128), F32),
        pltpu.VMEM((8, 4, 8, 128), F32),
        pltpu.VMEM((8, 4, 4, 8, 128), F32),
        pltpu.VMEM((256, 128), F32),
        pltpu.VMEM((1024, 128), F32),
        pltpu.VMEM((4, 256, 256), F32),
        pltpu.VMEM((3, 2, 512, 128), F32),
        pltpu.VMEM((512, 256), BF16),
        pltpu.VMEM((512, 256), BF16),
        pltpu.VMEM((2, 1024, 128), BF16),
        pltpu.VMEM((2, 1024, 128), BF16),
        pltpu.VMEM((1024, 128), F32),
        pltpu.VMEM((1024, 128), F32),
        pltpu.VMEM((1024, 128), F32),
        pltpu.VMEM((1024, 128), F32),
        pltpu.VMEM((4, 256, 128), F32),
        pltpu.VMEM((4, 256, 128), F32),
        pltpu.VMEM((256, 128), F32),
        pltpu.VMEM((256, 128), F32),
        pltpu.VMEM((8, 4, 8, 128), F32),
        pltpu.VMEM((8, 4, 8, 128), F32),
        pltpu.SemaphoreType.DMA((len(NAMES),)),
        pltpu.SemaphoreType.DMA((4,)),
        pltpu.SemaphoreType.DMA((14,)),
        pltpu.SemaphoreType.DMA((14,)),
    ]
    anywhere = pl.BlockSpec(memory_space=pl.ANY)
    block = pl.pallas_call(
        kernel,
        out_shape=jax.ShapeDtypeStruct((8, 4, 8, 128), F32),
        in_specs=[anywhere] * (4 + len(NAMES)),
        out_specs=pl.BlockSpec(memory_space=pltpu.VMEM),
        scratch_shapes=scratch,
        compiler_params=pltpu.CompilerParams(
            collective_id=0, has_side_effects=True, vmem_limit_bytes=56 * 1024 * 1024
        ),
        name="gradient",
    )(
        tiles(object_field),
        tiles(images[0]),
        tiles(transfer_real[0]).reshape(4, 256, 128),
        tiles(transfer_imaginary[0]).reshape(4, 256, 128),
        *operands,
    )
    return block.transpose(0, 2, 1, 3).reshape(64, 512)


def solution(mesh):
    placed = (
        P("row", "col"),
        P("frame", "row", "col"),
        P("frame", ("row", "col"), None),
        P("frame", ("row", "col"), None),
    )
    return jax.shard_map(
        shards, mesh=mesh, in_specs=placed, out_specs=P(("frame", "row"), "col"), check_vma=False
    )
```

```python
import functools
import math

import jax
import jax.numpy as jnp
import ml_dtypes
import numpy as np
from jax import lax
from jax.experimental import pallas as pl
from jax.experimental.pallas import tpu as pltpu
from jax.sharding import PartitionSpec as P

F32 = jnp.float32
BF16 = jnp.bfloat16
MESH = pl.DeviceIdType.MESH

N = 4096
DEVICES = 128


def block_of(g):
    return np.where(g < 64, 2 * g, 2 * (127 - g) + 1)


def halves(table):
    high = table.astype(np.float32).astype(ml_dtypes.bfloat16)
    low = (table - high.astype(np.float64)).astype(np.float32).astype(ml_dtypes.bfloat16)
    return high, low


def turn(numbers, length):
    angles = 2.0 * math.pi / length * (numbers % length)
    return np.cos(angles), np.sin(angles)


def vertical_forward(order):
    cosine, sine = turn(np.arange(512)[:, None] * order[None, :], 512)
    pieces = []
    for chunk in range(4):
        rows = slice(128 * chunk, 128 * chunk + 128)
        high, low = halves(np.concatenate([cosine[rows], -sine[rows]], 0))
        pieces += [high, low]
    return np.concatenate(pieces, 0)


def vertical_inverse(order):
    cosine, sine = turn(order[:, None] * np.arange(512)[None, :], 512)
    whole = np.concatenate([sine, cosine, -sine], 1)
    pieces = []
    for chunk in range(4):
        pieces += list(halves(whole[128 * chunk : 128 * chunk + 128]))
    return np.concatenate(pieces, 0)


def tables():
    made = {}
    g = np.arange(128)
    full = (4 * g[None, :] + np.arange(4)[:, None]).reshape(-1)
    f, r, c = np.meshgrid(np.arange(4), np.arange(16), np.arange(8), indexing="ij")
    made["down_object"] = vertical_forward((32 * r + 8 * f + c).reshape(-1))
    made["down_full"] = vertical_forward(full)
    made["up_full"] = vertical_inverse(full)
    made["up_gradient"] = vertical_inverse(np.arange(512))

    s, t = np.meshgrid(np.arange(16), np.arange(8), indexing="ij")
    s, t = s.reshape(-1), t.reshape(-1)
    sh, v1, sl = np.meshgrid(np.arange(2), np.arange(8), np.arange(8), indexing="ij")
    spectral_s, spectral_v = (8 * sh + sl).reshape(-1), v1.reshape(-1)
    cosine, sine = turn(t[:, None] * spectral_v[None, :], 8)
    same = (s[:, None] == spectral_s[None, :]).astype(np.float64)
    cosine, sine = cosine * same, sine * same
    made["mix_down"] = np.concatenate(halves(np.block([[cosine, -sine], [sine, cosine]])), 0)
    made["mix_up"] = np.concatenate(halves(np.block([[cosine.T, sine.T], [-sine.T, cosine.T]])), 0)
    cosine, sine = turn(np.arange(512)[:, None] * t[None, :], 4096)
    made["twist_vertical"] = np.concatenate([cosine, sine], 0).astype(np.float32)

    x1, tx = s, t
    same = (t[:, None] == tx[None, :]).astype(np.float64)
    cosine, sine = turn(s[:, None] * x1[None, :], 16)
    cosine, sine = cosine * same, sine * same
    made["open_x"] = np.concatenate(halves(np.concatenate([cosine, -sine], 0)), 0)
    scale = 1.0 / (float(N) * float(N))
    made["close_x"] = np.concatenate(halves(np.concatenate([cosine.T, -sine.T], 1) * scale), 0)
    cosine, sine = turn(s[:, None] * np.arange(256)[None, :], 4096)
    made["twist_out"] = np.concatenate([cosine, sine], 0).astype(np.float32)
    made["twist_in"] = np.concatenate([cosine.T, sine.T], 0).astype(np.float32)

    cosine, sine = turn(block_of(g)[:, None] * np.arange(256)[None, :], 256)
    alternate = np.zeros((16, 512))
    alternate[0, :256] = 1.0 - 2.0 * (np.arange(256) % 2)
    whole = np.block([[cosine, sine], [-sine, cosine]])
    made["across"] = np.concatenate(halves(np.concatenate([whole, alternate], 0)), 0)
    cosine, sine = turn(np.arange(256)[:, None] * block_of(g)[None, :], 256)
    made["back_x"] = np.concatenate(halves(np.block([[cosine, -sine], [sine, cosine]])), 0)

    choose = np.zeros((3, 384, 512))
    for kind in range(3):
        for row in range(128):
            slot, v = spectral_s[row], spectral_v[row]

            def own(number):
                return (number // 8) * 64 + v * 8 + number % 8

            def got(number):
                return 256 + (number // 8) * 64 + v * 8 + number % 8

            extra = 384 + v
            if kind == 2:
                plus, minus = got(slot), own(16 - slot)
            else:
                plus, minus = own(slot), (extra if slot == 0 else got(16 - slot))
            if kind == 0 and slot == 0:
                choose[kind, row, plus] = 1.0
                choose[kind, 128 + row, minus] = 1.0
            else:
                for part, sign in ((0, 1.0), (128, 1.0), (256, -1.0)):
                    choose[kind, part + row, plus] = 1.0
                    choose[kind, part + row, minus] = sign
    made["choose"] = choose.astype(ml_dtypes.bfloat16)
    return made


def product(left, right):
    return lax.dot_general(left, right, (((1,), (0,)), ((), ())), preferred_element_type=F32)


def product_turned(left, right):
    return lax.dot_general(left, right, (((1,), (1,)), ((), ())), preferred_element_type=F32)


def split(values):
    high = values.astype(BF16)
    return high, (values - high.astype(F32)).astype(BF16)


def table_first(table, high, low, dot):
    rows = table.shape[0] // 2
    both = dot(table, high)
    return both[:rows] + (both[rows:] + dot(table[:rows], low))


def table_last(values, table):
    depth = table.shape[0] // 2
    rows = values.shape[0]
    high, low = split(values)
    both = product(jnp.concatenate([high, low], 0), table[:depth])
    return both[:rows] + (both[rows:] + product(high, table[depth:]))


def rows_to_half(fields, tab):
    opened = table_first(tab["open_x"][...], *split(jnp.concatenate(fields, 1)), product)
    cosine, sine = tab["twist_out"][:128, :], tab["twist_out"][128:, :]
    turned = []
    for number in range(len(fields)):
        part = slice(256 * number, 256 * number + 256)
        real, imaginary = opened[:128, part], opened[128:, part]
        turned.append(
            jnp.concatenate(
                [real * cosine + imaginary * sine, imaginary * cosine - real * sine], 1
            )
        )
    out = table_first(tab["across"][...], *split(jnp.concatenate(turned, 0)), product_turned)
    row = lax.broadcasted_iota(jnp.int32, (128, 128), 0)
    lane = lax.broadcasted_iota(jnp.int32, (128, 128), 1)
    shared = (row == 0) & (lane < 8)
    pairs = []
    for number in range(len(fields)):
        part = slice(128 * number, 128 * number + 128)
        extra = jnp.where(shared, out[256:257, part], 0.0)
        pairs.append((out[:128, part], out[128:256, part] + extra))
    return pairs


def half_to_rows(planes, tab):
    back = table_first(tab["back_x"][...], *split(jnp.concatenate(planes, 1)), product)
    lane = lax.broadcasted_iota(jnp.int32, (256, 128), 1)
    number = lax.broadcasted_iota(jnp.int32, (256, 128), 0)
    cosine, sine = tab["twist_in"][:256, :], tab["twist_in"][256:, :]
    fields = []
    for which, plane in enumerate(planes):
        part = slice(128 * which, 128 * which + 128)
        shared = jnp.where(lane < 8, plane[128:129], 0.0)
        real = back[:256, part] + jnp.where(number % 2 == 0, shared, -shared)
        imaginary = back[256:, part]
        turned = jnp.concatenate(
            [real * cosine - imaginary * sine, real * sine + imaginary * cosine], 1
        )
        fields.append(table_first(tab["close_x"][...], *split(turned), product_turned))
    return fields


def down_chunk(opened, cosine, sine, tab):
    real, imaginary = opened[:128], opened[128:]
    cosine = jnp.concatenate([cosine, cosine], 1)
    sine = jnp.concatenate([sine, sine], 1)
    turned_real = real * cosine + imaginary * sine
    turned_imaginary = imaginary * cosine - real * sine
    stacked = jnp.concatenate(
        [
            jnp.concatenate([turned_real[:, :128], turned_imaginary[:, :128]], 1),
            jnp.concatenate([turned_real[:, 128:], turned_imaginary[:, 128:]], 1),
        ],
        0,
    )
    return table_last(stacked, tab["mix_down"][...])


def up_chunk(mixed, cosine, sine, tab, weights, conjugate):
    ar, ai = mixed[:128, :128], mixed[:128, 128:]
    br, bi = mixed[128:, :128], mixed[128:, 128:]
    (s1r, s1i), (s2r, s2i), (dr, di) = weights
    if conjugate:
        s1i, s2i, di = -s1i, -s2i, -di
    ur = s1r * ar - s1i * ai - (dr * bi + di * br)
    ui = s1r * ai + s1i * ar + (dr * br - di * bi)
    vr = dr * ar - di * ai - (s2r * bi + s2i * br)
    vi = dr * ai + di * ar + (s2r * br - s2i * bi)
    stacked = jnp.concatenate(
        [jnp.concatenate([ur, ui], 1), jnp.concatenate([vr, vi], 1)], 0
    )
    mixed = table_last(stacked, tab["mix_up"][...])
    cosine = jnp.concatenate([cosine, cosine], 0)
    sine = jnp.concatenate([sine, sine], 0)
    real, imaginary = mixed[:, :128], mixed[:, 128:]
    return real * cosine - imaginary * sine, real * sine + imaginary * cosine


NAMES = (
    "open_x",
    "twist_out",
    "across",
    "down_object",
    "twist_vertical",
    "mix_down",
    "choose",
    "mix_up",
    "up_full",
    "back_x",
    "twist_in",
    "close_x",
    "down_full",
    "up_gradient",
)


def kernel(*refs):
    object_ref, images_ref, real_ref, imaginary_ref = refs[:4]
    sources = refs[4 : 4 + len(NAMES)]
    out_ref = refs[4 + len(NAMES)]
    rest = refs[5 + len(NAMES) :]
    tab = dict(zip(NAMES, rest[: len(NAMES)]))
    (
        transfer,
        partner,
        extra_send,
        extra,
        object_rows,
        image_rows,
        send_a,
        pencils,
        middle,
        weight,
        split_high,
        split_low,
        back_high,
        back_low,
        send_four,
        got_four,
        send_five,
        got_five,
        send_six,
        got_six,
        send_c,
        got_d,
        send_out,
        got_out,
        table_sem,
        local_sem,
        send_sem,
        recv_sem,
    ) = rest[len(NAMES) :]

    frame, row, col = lax.axis_index("frame"), lax.axis_index("row"), lax.axis_index("col")
    me = row * 8 + col

    loads = {
        name: pltpu.make_async_copy(source, tab[name], table_sem.at[number])
        for number, (name, source) in enumerate(zip(NAMES, sources))
    }

    def need(*names):
        for name in names:
            loads[name].wait()

    transfer_loads = [
        pltpu.make_async_copy(real_ref, transfer.at[0], local_sem.at[0]),
        pltpu.make_async_copy(imaginary_ref, transfer.at[1], local_sem.at[1]),
    ]
    object_load = pltpu.make_async_copy(
        object_ref.at[8 * frame + col], object_rows.at[col], local_sem.at[2]
    )
    images_load = pltpu.make_async_copy(
        images_ref.at[pl.ds(4 * col, 4)], image_rows.at[col], local_sem.at[3]
    )
    for load in transfer_loads:
        load.start()
    object_load.start()
    images_load.start()
    for name in NAMES:
        loads[name].start()

    barrier = pltpu.get_barrier_semaphore()

    columns = [lax.rem(col + number, 8) for number in range(8)]

    def each_peer(body):
        for first, last in ((8, 12), (12, 16), (4, 8), (1, 4)):

            def step(number, carry):
                r = lax.rem(row + number, 16)
                for c in columns:
                    body(r, c)
                return carry

            lax.fori_loop(first, last, step, 0)
        for c in columns[1:]:
            body(row, c)

    opposite = 127 - me
    is_end = 1 - (lax.rem(me, 64) + 63) // 64
    beyond = 128 - me - 64 * is_end
    mirror = (frame, opposite // 8, lax.rem(opposite, 8))
    after = (frame, beyond // 8, lax.rem(beyond, 8))

    def greet(device):
        pl.semaphore_signal(barrier, inc=1, device_id=device, device_id_type=MESH)

    greet(mirror)
    greet(after)
    for c in columns[1:]:
        greet((frame, row, c))

    def greet_row(number, carry):
        greet((frame, lax.rem(row + number, 16), col))
        return carry

    lax.fori_loop(1, 16, greet_row, 0)
    for step in range(1, 4):
        greet((lax.rem(frame + step, 4), row, col))
    pl.semaphore_wait(barrier, 2 + 7 + 15 + 3)

    def send(source, target, phase, device):
        pltpu.make_async_remote_copy(
            src_ref=source,
            dst_ref=target,
            send_sem=send_sem.at[phase],
            recv_sem=recv_sem.at[phase],
            device_id=device,
            device_id_type=MESH,
        ).start()

    def wait_bytes(like, semaphore):
        pltpu.make_async_copy(like, like, semaphore).wait()

    def each_col(body):
        for c in columns[1:]:
            body(c)

    def each_frame(body):
        for number in range(1, 4):
            body(lax.rem(frame + number, 4))

    def block(number, size):
        return pl.ds(pl.multiple_of(number * size, size), size)

    each_col(
        lambda c: send(
            object_ref.at[8 * frame + c], object_rows.at[col], 0, (frame, row, c)
        )
    )
    for load in transfer_loads:
        load.wait()
    for plane in range(2):
        extra_send[plane] = transfer[plane, 0, pl.ds(0, 32, stride=8), :]
    def send_partner(number):
        plane, a, part = number // 8, lax.rem(number // 4, 2), lax.rem(number, 4)
        rows = block(part, 64)
        send(transfer.at[plane, 2 + a, rows], partner.at[plane, a, rows], 3, mirror)

    def send_image(c):
        send(images_ref.at[pl.ds(4 * c, 4)], image_rows.at[col], 1, (frame, row, c))

    for number in range(6):
        send_partner(number)

    def field_of(read):
        return jnp.concatenate(
            [
                jnp.concatenate([read(x1 // 2, 2 * (x1 % 2) + part) for x1 in range(16)], 0)
                for part in range(2)
            ],
            1,
        )

    def to_all(source, target, size, phase):
        target[block(me, size), :] = source[block(me, size), :]
        own = block(me, size)
        each_peer(
            lambda r, c: send(
                source.at[block(r * 8 + c, size)], target.at[own], phase, (frame, r, c)
            )
        )

    object_load.wait()
    wait_bytes(object_rows.at[pl.ds(0, 7)], recv_sem.at[0])
    need("open_x", "twist_out", "across")
    planes = rows_to_half([field_of(lambda c, k: object_rows[c, k])], tab)[0]
    for plane in range(2):
        send_a[pl.ds(plane, 128, stride=2), :] = planes[plane]
    quarter = pencils.at[block(frame, 256)]
    quarter[block(me, 2), :] = send_a[block(me, 2), :]

    def send_pencil(r, c):
        send(send_a.at[block(r * 8 + c, 2)], quarter.at[block(me, 2)], 5, (frame, r, c))

    def some_rows(step, carry):
        for number in range(5):
            for c in columns:
                send_pencil(lax.rem(row + 1 + lax.rem(6 + 5 * step + number, 15), 16), c)
        return carry

    for c in columns[1:]:
        send_pencil(row, c)
    lax.fori_loop(0, 3, some_rows, 0)
    send(extra_send, extra, 2, after)
    for number in range(6, 16):
        send_partner(number)
        if number >= 9:
            send_image(columns[number - 8])
    wait_bytes(send_a.at[pl.ds(0, 254)], recv_sem.at[5])
    each_frame(lambda f: send(quarter, quarter, 7, (f, row, col)))
    wait_bytes(pencils.at[pl.ds(0, 768)], recv_sem.at[7])

    def turns(number):
        return (
            tab["twist_vertical"][pl.ds(128 * number, 128), :],
            tab["twist_vertical"][pl.ds(512 + 128 * number, 128), :],
        )

    def opened(name, number, rows):
        return table_first(
            tab[name][pl.ds(512 * number, 512), rows], split_high[rows], split_low[rows], product
        )

    def up(mixed, number, conjugate):
        rows = pl.ds(128 * number, 128)
        weights = [(weight[k, 0, rows, :], weight[k, 1, rows, :]) for k in range(3)]
        planes = up_chunk(mixed, *turns(number), tab, weights, conjugate)
        for plane, values in enumerate(planes):
            high, low = split(values)
            for which in range(2):
                part = slice(128 * which, 128 * which + 128)
                at = pl.ds(512 * plane + 128 * number, 128)
                back_high[which, at, :] = high[part]
                back_low[which, at, :] = low[part]

    for plane in range(2):
        high, low = split(pencils[pl.ds(plane, 512, stride=2), :])
        split_high[:, 128 * plane : 128 * plane + 128] = high
        split_low[:, 128 * plane : 128 * plane + 128] = low
    need("down_object", "twist_vertical", "mix_down")
    for number in range(4):
        middle[number] = down_chunk(
            opened("down_object", number, slice(0, 512)), *turns(number), tab
        )

    wait_bytes(extra, recv_sem.at[2])
    wait_bytes(partner, recv_sem.at[3])
    need("choose")
    kind = (me + 127) // 128 + me // 64
    for part in range(4):
        blocks = []
        for plane in range(2):
            rows = [
                transfer[plane, a, pl.ds((4 * v + part) * 8, 8), :]
                for a in range(4)
                for v in range(8)
            ]
            rows += [
                partner[plane, a, pl.ds((4 * v + part) * 8, 8), :]
                for a in range(2)
                for v in range(8)
            ]
            rows += [extra[plane, pl.ds(part, 8, stride=4), :], jnp.zeros((120, 128), F32)]
            blocks.append(jnp.concatenate(rows, 0))
        gathered = jnp.concatenate(blocks, 1)
        first = gathered.astype(BF16)
        left = gathered - first.astype(F32)
        second = left.astype(BF16)
        third = (left - second.astype(F32)).astype(BF16)
        chosen = tab["choose"][kind]
        picked = product(chosen, first) + (product(chosen, second) + product(chosen, third))
        for number in range(3):
            for plane in range(2):
                weight[number, plane, pl.ds(128 * part, 128), :] = picked[
                    128 * number : 128 * number + 128, 128 * plane : 128 * plane + 128
                ].T

    def return_chunk(name, number):
        table = tab[name][block(number, 256), :]
        real = table_first(table[:, 512:], back_high[0], back_low[0], product)
        imaginary = table_first(table[:, :1024], back_high[1], back_low[1], product)
        return real, imaginary

    need("mix_up")
    for number in range(4):
        up(middle[number], number, False)
    need("up_full")
    for half in range(2):
        for number in range(2):
            planes = return_chunk("up_full", 2 * half + number)
            for plane in range(2):
                send_four[half, pl.ds(2 * plane + number, 128, stride=4), :] = planes[plane]
        if half == 1:
            wait_bytes(got_four.at[0, pl.ds(0, 127 * 4)], send_sem.at[8])
        to_all(send_four.at[half], got_four.at[half], 4, 8 + half)

    images_load.wait()
    wait_bytes(image_rows.at[pl.ds(0, 7)], recv_sem.at[1])
    need("back_x", "twist_in", "close_x")
    for half in range(2):
        wait_bytes(got_four.at[half, pl.ds(0, 127 * 4)], recv_sem.at[8 + half])
        modelled = half_to_rows(
            [
                jnp.concatenate(
                    [
                        got_four[half, pl.ds(number, 128, stride=4), :],
                        got_four[half, pl.ds(2 + number, 128, stride=4), :],
                    ],
                    0,
                )
                for number in range(2)
            ],
            tab,
        )
        weighted = []
        for number, model in enumerate(modelled):
            images = field_of(lambda c, k: image_rows[c, 2 * half + number, k])
            weighted.append((model - images) / (0.5 + jnp.abs(images)))
        for number, planes in enumerate(rows_to_half(weighted, tab)):
            for plane in range(2):
                send_five[half, pl.ds(2 * plane + number, 128, stride=4), :] = planes[plane]
        to_all(send_five.at[half], got_five.at[half], 4, 14 + half)

    need("down_full", "up_gradient")
    for half in range(2):
        wait_bytes(got_five.at[half, pl.ds(0, 127 * 4)], recv_sem.at[14 + half])
        for plane in range(2):
            for number in range(2):
                high, low = split(got_five[half, pl.ds(2 * plane + number, 128, stride=4), :])
                first = 256 * half + 128 * number
                at = (slice(first, first + 128), slice(128 * plane, 128 * plane + 128))
                split_high[at] = high
                split_low[at] = low
        if half == 0:
            for number in range(4):
                middle[number] = opened("down_full", number, slice(0, 256))
    for number in range(4):
        whole = middle[number] + opened("down_full", number, slice(256, 512))
        up(down_chunk(whole, *turns(number), tab), number, True)

    near = row // 8
    parts = [block(near, 128), block(1 - near, 128)]
    for step in (2, 1, 3, 0):
        f = lax.rem(frame + step, 4)
        planes = return_chunk("up_gradient", f)
        target = got_six if step == 0 else send_six
        for plane in range(2):
            target[f, pl.ds(plane, 128, stride=2), :] = planes[plane]
        if step > 0:
            send(send_six.at[f, parts[0]], got_six.at[frame, parts[0]], 4, (f, row, col))
    for step in (2, 1, 3):
        f = lax.rem(frame + step, 4)
        send(send_six.at[f, parts[1]], got_six.at[frame, parts[1]], 10, (f, row, col))
    for half in range(2):
        wait_bytes(send_six.at[pl.ds(0, 3), pl.ds(0, 128)], recv_sem.at[4 if half == 0 else 10])
        pieces = [got_six[f, parts[half], :] for f in range(4)]
        send_c[parts[half], :] = (pieces[0] + pieces[1]) + (pieces[2] + pieces[3])
        first = 8 * near if half == 0 else 8 - 8 * near

        def send_quarter(r, c):
            send(send_c.at[block(r * 8 + c, 2)], got_d.at[block(me, 2)], 11, (frame, r, c))

        def some_rows(number, carry):
            for c in columns:
                send_quarter(first + lax.rem(row + number, 8), c)
            return carry

        if half == 0:
            got_d[block(me, 2), :] = send_c[block(me, 2), :]
            for c in columns[1:]:
                send_quarter(row, c)
        lax.fori_loop(1 - half, 8, some_rows, 0)
    wait_bytes(send_c.at[pl.ds(0, 254)], recv_sem.at[11])
    field = half_to_rows(
        [jnp.concatenate([got_d[pl.ds(0, 128, stride=2), :], got_d[pl.ds(1, 128, stride=2), :]], 0)],
        tab,
    )[0]
    for x1 in range(16):
        for part in range(2):
            send_out[x1 // 2, 2 * (x1 % 2) + part] = field[
                8 * x1 : 8 * x1 + 8, 128 * part : 128 * part + 128
            ]
    got_out[col] = send_out[col]
    each_col(lambda c: send(send_out.at[c], got_out.at[col], 13, (frame, row, c)))
    wait_bytes(send_out.at[pl.ds(0, 7)], recv_sem.at[13])
    out_ref[...] = got_out[...]

    wait_bytes(object_rows.at[pl.ds(0, 7)], send_sem.at[0])
    wait_bytes(image_rows.at[pl.ds(0, 7)], send_sem.at[1])
    wait_bytes(extra, send_sem.at[2])
    wait_bytes(partner, send_sem.at[3])
    wait_bytes(send_a.at[pl.ds(0, 254)], send_sem.at[5])
    wait_bytes(pencils.at[pl.ds(0, 768)], send_sem.at[7])
    wait_bytes(got_four.at[1, pl.ds(0, 127 * 4)], send_sem.at[9])
    for half in range(2):
        wait_bytes(got_five.at[half, pl.ds(0, 127 * 4)], send_sem.at[14 + half])
    wait_bytes(send_six.at[pl.ds(0, 3), pl.ds(0, 128)], send_sem.at[4])
    wait_bytes(send_six.at[pl.ds(0, 3), pl.ds(0, 128)], send_sem.at[10])
    wait_bytes(send_c.at[pl.ds(0, 254)], send_sem.at[11])
    wait_bytes(send_out.at[pl.ds(0, 7)], send_sem.at[13])


def tiles(block):
    rows, columns = block.shape
    return block.reshape(rows // 8, 8, columns // 128, 128).transpose(0, 2, 1, 3)


def shards(object_field, images, transfer_real, transfer_imaginary):
    made = tables()
    operands = [made[name] for name in NAMES]
    scratch = [pltpu.VMEM(table.shape, table.dtype) for table in operands]
    scratch += [
        pltpu.VMEM((2, 4, 256, 128), F32),
        pltpu.VMEM((2, 2, 256, 128), F32),
        pltpu.VMEM((2, 32, 128), F32),
        pltpu.VMEM((2, 32, 128), F32),
        pltpu.VMEM((8, 4, 8, 128), F32),
        pltpu.VMEM((8, 4, 4, 8, 128), F32),
        pltpu.VMEM((256, 128), F32),
        pltpu.VMEM((1024, 128), F32),
        pltpu.VMEM((4, 256, 256), F32),
        pltpu.VMEM((3, 2, 512, 128), F32),
        pltpu.VMEM((512, 256), BF16),
        pltpu.VMEM((512, 256), BF16),
        pltpu.VMEM((2, 1024, 128), BF16),
        pltpu.VMEM((2, 1024, 128), BF16),
        pltpu.VMEM((2, 512, 128), F32),
        pltpu.VMEM((2, 512, 128), F32),
        pltpu.VMEM((2, 512, 128), F32),
        pltpu.VMEM((2, 512, 128), F32),
        pltpu.VMEM((4, 256, 128), F32),
        pltpu.VMEM((4, 256, 128), F32),
        pltpu.VMEM((256, 128), F32),
        pltpu.VMEM((256, 128), F32),
        pltpu.VMEM((8, 4, 8, 128), F32),
        pltpu.VMEM((8, 4, 8, 128), F32),
        pltpu.SemaphoreType.DMA((len(NAMES),)),
        pltpu.SemaphoreType.DMA((4,)),
        pltpu.SemaphoreType.DMA((16,)),
        pltpu.SemaphoreType.DMA((16,)),
    ]
    anywhere = pl.BlockSpec(memory_space=pl.ANY)
    block = pl.pallas_call(
        kernel,
        out_shape=jax.ShapeDtypeStruct((8, 4, 8, 128), F32),
        in_specs=[anywhere] * (4 + len(NAMES)),
        out_specs=pl.BlockSpec(memory_space=pltpu.VMEM),
        scratch_shapes=scratch,
        compiler_params=pltpu.CompilerParams(
            collective_id=0, has_side_effects=True, vmem_limit_bytes=56 * 1024 * 1024
        ),
        name="gradient",
    )(
        tiles(object_field),
        tiles(images[0]),
        tiles(transfer_real[0]).reshape(4, 256, 128),
        tiles(transfer_imaginary[0]).reshape(4, 256, 128),
        *operands,
    )
    return block.transpose(0, 2, 1, 3).reshape(64, 512)


def solution(mesh):
    placed = (
        P("row", "col"),
        P("frame", "row", "col"),
        P("frame", ("row", "col"), None),
        P("frame", ("row", "col"), None),
    )
    return jax.shard_map(
        shards, mesh=mesh, in_specs=placed, out_specs=P(("frame", "row"), "col"), check_vma=False
    )
```

```python
import functools
import math

import jax
import jax.numpy as jnp
import ml_dtypes
import numpy as np
from jax import lax
from jax.experimental import pallas as pl
from jax.experimental.pallas import tpu as pltpu
from jax.sharding import PartitionSpec as P

F32 = jnp.float32
BF16 = jnp.bfloat16
MESH = pl.DeviceIdType.MESH

N = 4096
DEVICES = 128


def block_of(g):
    return np.where(g < 64, 2 * g, 2 * (127 - g) + 1)


def halves(table):
    high = table.astype(np.float32).astype(ml_dtypes.bfloat16)
    low = (table - high.astype(np.float64)).astype(np.float32).astype(ml_dtypes.bfloat16)
    return high, low


def turn(numbers, length):
    angles = 2.0 * math.pi / length * (numbers % length)
    return np.cos(angles), np.sin(angles)


def vertical_forward(order):
    cosine, sine = turn(np.arange(512)[:, None] * order[None, :], 512)
    pieces = []
    for chunk in range(4):
        rows = slice(128 * chunk, 128 * chunk + 128)
        high, low = halves(np.concatenate([cosine[rows], -sine[rows]], 0))
        pieces += [high, low]
    return np.concatenate(pieces, 0)


def vertical_inverse(order):
    cosine, sine = turn(order[:, None] * np.arange(512)[None, :], 512)
    whole = np.concatenate([sine, cosine, -sine], 1)
    pieces = []
    for chunk in range(4):
        pieces += list(halves(whole[128 * chunk : 128 * chunk + 128]))
    return np.concatenate(pieces, 0)


def tables():
    made = {}
    g = np.arange(128)
    full = (4 * g[None, :] + np.arange(4)[:, None]).reshape(-1)
    f, r, c = np.meshgrid(np.arange(4), np.arange(16), np.arange(8), indexing="ij")
    made["down_object"] = vertical_forward((32 * r + 8 * f + c).reshape(-1))
    made["down_full"] = vertical_forward(full)
    made["up_full"] = vertical_inverse(full)
    made["up_gradient"] = vertical_inverse(np.arange(512))

    s, t = np.meshgrid(np.arange(16), np.arange(8), indexing="ij")
    s, t = s.reshape(-1), t.reshape(-1)
    sh, v1, sl = np.meshgrid(np.arange(2), np.arange(8), np.arange(8), indexing="ij")
    spectral_s, spectral_v = (8 * sh + sl).reshape(-1), v1.reshape(-1)
    cosine, sine = turn(t[:, None] * spectral_v[None, :], 8)
    same = (s[:, None] == spectral_s[None, :]).astype(np.float64)
    cosine, sine = cosine * same, sine * same
    made["mix_down"] = np.concatenate(halves(np.block([[cosine, -sine], [sine, cosine]])), 0)
    made["mix_up"] = np.concatenate(halves(np.block([[cosine.T, sine.T], [-sine.T, cosine.T]])), 0)
    cosine, sine = turn(np.arange(512)[:, None] * t[None, :], 4096)
    made["twist_vertical"] = np.concatenate([cosine, sine], 0).astype(np.float32)

    x1, tx = s, t
    same = (t[:, None] == tx[None, :]).astype(np.float64)
    cosine, sine = turn(s[:, None] * x1[None, :], 16)
    cosine, sine = cosine * same, sine * same
    made["open_x"] = np.concatenate(halves(np.concatenate([cosine, -sine], 0)), 0)
    scale = 1.0 / (float(N) * float(N))
    made["close_x"] = np.concatenate(halves(np.concatenate([cosine.T, -sine.T], 1) * scale), 0)
    cosine, sine = turn(s[:, None] * np.arange(256)[None, :], 4096)
    made["twist_out"] = np.concatenate([cosine, sine], 0).astype(np.float32)
    made["twist_in"] = np.concatenate([cosine.T, sine.T], 0).astype(np.float32)

    cosine, sine = turn(block_of(g)[:, None] * np.arange(256)[None, :], 256)
    alternate = np.zeros((16, 512))
    alternate[0, :256] = 1.0 - 2.0 * (np.arange(256) % 2)
    whole = np.block([[cosine, sine], [-sine, cosine]])
    made["across"] = np.concatenate(halves(np.concatenate([whole, alternate], 0)), 0)
    cosine, sine = turn(np.arange(256)[:, None] * block_of(g)[None, :], 256)
    made["back_x"] = np.concatenate(halves(np.block([[cosine, -sine], [sine, cosine]])), 0)

    choose = np.zeros((3, 384, 512))
    for kind in range(3):
        for row in range(128):
            slot, v = spectral_s[row], spectral_v[row]

            def own(number):
                return (number // 8) * 64 + v * 8 + number % 8

            def got(number):
                return 256 + (number // 8) * 64 + v * 8 + number % 8

            extra = 384 + v
            if kind == 2:
                plus, minus = got(slot), own(16 - slot)
            else:
                plus, minus = own(slot), (extra if slot == 0 else got(16 - slot))
            if kind == 0 and slot == 0:
                choose[kind, row, plus] = 1.0
                choose[kind, 128 + row, minus] = 1.0
            else:
                for part, sign in ((0, 1.0), (128, 1.0), (256, -1.0)):
                    choose[kind, part + row, plus] = 1.0
                    choose[kind, part + row, minus] = sign
    made["choose"] = choose.astype(ml_dtypes.bfloat16)
    return made


def product(left, right):
    return lax.dot_general(left, right, (((1,), (0,)), ((), ())), preferred_element_type=F32)


def product_turned(left, right):
    return lax.dot_general(left, right, (((1,), (1,)), ((), ())), preferred_element_type=F32)


def split(values):
    high = values.astype(BF16)
    return high, (values - high.astype(F32)).astype(BF16)


def table_first(table, high, low, dot):
    rows = table.shape[0] // 2
    both = dot(table, high)
    return both[:rows] + (both[rows:] + dot(table[:rows], low))


def table_last(values, table):
    depth = table.shape[0] // 2
    rows = values.shape[0]
    high, low = split(values)
    both = product(jnp.concatenate([high, low], 0), table[:depth])
    return both[:rows] + (both[rows:] + product(high, table[depth:]))


def rows_to_half(fields, tab):
    opened = table_first(tab["open_x"][...], *split(jnp.concatenate(fields, 1)), product)
    cosine, sine = tab["twist_out"][:128, :], tab["twist_out"][128:, :]
    turned = []
    for number in range(len(fields)):
        part = slice(256 * number, 256 * number + 256)
        real, imaginary = opened[:128, part], opened[128:, part]
        turned.append(
            jnp.concatenate(
                [real * cosine + imaginary * sine, imaginary * cosine - real * sine], 1
            )
        )
    out = table_first(tab["across"][...], *split(jnp.concatenate(turned, 0)), product_turned)
    row = lax.broadcasted_iota(jnp.int32, (128, 128), 0)
    lane = lax.broadcasted_iota(jnp.int32, (128, 128), 1)
    shared = (row == 0) & (lane < 8)
    pairs = []
    for number in range(len(fields)):
        part = slice(128 * number, 128 * number + 128)
        extra = jnp.where(shared, out[256:257, part], 0.0)
        pairs.append((out[:128, part], out[128:256, part] + extra))
    return pairs


def half_to_rows(planes, tab):
    back = table_first(tab["back_x"][...], *split(jnp.concatenate(planes, 1)), product)
    lane = lax.broadcasted_iota(jnp.int32, (256, 128), 1)
    number = lax.broadcasted_iota(jnp.int32, (256, 128), 0)
    cosine, sine = tab["twist_in"][:256, :], tab["twist_in"][256:, :]
    fields = []
    for which, plane in enumerate(planes):
        part = slice(128 * which, 128 * which + 128)
        shared = jnp.where(lane < 8, plane[128:129], 0.0)
        real = back[:256, part] + jnp.where(number % 2 == 0, shared, -shared)
        imaginary = back[256:, part]
        turned = jnp.concatenate(
            [real * cosine - imaginary * sine, real * sine + imaginary * cosine], 1
        )
        fields.append(table_first(tab["close_x"][...], *split(turned), product_turned))
    return fields


def down_chunk(opened, cosine, sine, tab):
    real, imaginary = opened[:128], opened[128:]
    cosine = jnp.concatenate([cosine, cosine], 1)
    sine = jnp.concatenate([sine, sine], 1)
    turned_real = real * cosine + imaginary * sine
    turned_imaginary = imaginary * cosine - real * sine
    stacked = jnp.concatenate(
        [
            jnp.concatenate([turned_real[:, :128], turned_imaginary[:, :128]], 1),
            jnp.concatenate([turned_real[:, 128:], turned_imaginary[:, 128:]], 1),
        ],
        0,
    )
    return table_last(stacked, tab["mix_down"][...])


def up_chunk(mixed, cosine, sine, tab, weights, conjugate):
    ar, ai = mixed[:128, :128], mixed[:128, 128:]
    br, bi = mixed[128:, :128], mixed[128:, 128:]
    (s1r, s1i), (s2r, s2i), (dr, di) = weights
    if conjugate:
        s1i, s2i, di = -s1i, -s2i, -di
    ur = s1r * ar - s1i * ai - (dr * bi + di * br)
    ui = s1r * ai + s1i * ar + (dr * br - di * bi)
    vr = dr * ar - di * ai - (s2r * bi + s2i * br)
    vi = dr * ai + di * ar + (s2r * br - s2i * bi)
    stacked = jnp.concatenate(
        [jnp.concatenate([ur, ui], 1), jnp.concatenate([vr, vi], 1)], 0
    )
    mixed = table_last(stacked, tab["mix_up"][...])
    cosine = jnp.concatenate([cosine, cosine], 0)
    sine = jnp.concatenate([sine, sine], 0)
    real, imaginary = mixed[:, :128], mixed[:, 128:]
    return real * cosine - imaginary * sine, real * sine + imaginary * cosine


NAMES = (
    "open_x",
    "twist_out",
    "across",
    "down_object",
    "twist_vertical",
    "mix_down",
    "choose",
    "mix_up",
    "up_full",
    "back_x",
    "twist_in",
    "close_x",
    "down_full",
    "up_gradient",
)


def kernel(*refs):
    object_ref, images_ref, real_ref, imaginary_ref = refs[:4]
    sources = refs[4 : 4 + len(NAMES)]
    out_ref = refs[4 + len(NAMES)]
    rest = refs[5 + len(NAMES) :]
    tab = dict(zip(NAMES, rest[: len(NAMES)]))
    (
        transfer,
        partner,
        extra_send,
        extra,
        object_rows,
        image_rows,
        send_a,
        pencils,
        middle,
        weight,
        split_high,
        split_low,
        back_high,
        back_low,
        send_four,
        got_four,
        send_five,
        got_five,
        send_six,
        got_six,
        send_c,
        got_d,
        send_out,
        got_out,
        table_sem,
        local_sem,
        send_sem,
        recv_sem,
    ) = rest[len(NAMES) :]

    frame, row, col = lax.axis_index("frame"), lax.axis_index("row"), lax.axis_index("col")
    me = row * 8 + col
    barrier = pltpu.get_barrier_semaphore()
    columns = [lax.rem(col + number, 8) for number in range(8)]

    opposite = 127 - me
    is_end = 1 - (lax.rem(me, 64) + 63) // 64
    beyond = 128 - me - 64 * is_end
    mirror = (frame, opposite // 8, lax.rem(opposite, 8))
    after = (frame, beyond // 8, lax.rem(beyond, 8))

    def greet(device):
        pl.semaphore_signal(barrier, inc=1, device_id=device, device_id_type=MESH)

    greet(mirror)
    greet(after)
    for c in columns[1:]:
        greet((frame, row, c))

    def greet_row(number, carry):
        greet((frame, lax.rem(row + number, 16), col))
        return carry

    lax.fori_loop(1, 16, greet_row, 0)
    for step in range(1, 4):
        greet((lax.rem(frame + step, 4), row, col))

    loads = {
        name: pltpu.make_async_copy(source, tab[name], table_sem.at[number])
        for number, (name, source) in enumerate(zip(NAMES, sources))
    }

    def need(*names):
        for name in names:
            loads[name].wait()

    transfer_loads = [
        pltpu.make_async_copy(real_ref, transfer.at[0], local_sem.at[0]),
        pltpu.make_async_copy(imaginary_ref, transfer.at[1], local_sem.at[1]),
    ]
    object_load = pltpu.make_async_copy(
        object_ref.at[8 * frame + col], object_rows.at[col], local_sem.at[2]
    )
    images_load = pltpu.make_async_copy(
        images_ref.at[pl.ds(4 * col, 4)], image_rows.at[col], local_sem.at[3]
    )
    for load in transfer_loads:
        load.start()
    object_load.start()
    images_load.start()
    for name in NAMES:
        loads[name].start()


    def each_peer(body):
        for first, last in ((8, 12), (12, 16), (4, 8), (1, 4)):

            def step(number, carry):
                r = lax.rem(row + number, 16)
                for c in columns:
                    body(r, c)
                return carry

            lax.fori_loop(first, last, step, 0)
        for c in columns[1:]:
            body(row, c)

    pl.semaphore_wait(barrier, 2 + 7 + 15 + 3)

    def send(source, target, phase, device):
        pltpu.make_async_remote_copy(
            src_ref=source,
            dst_ref=target,
            send_sem=send_sem.at[phase],
            recv_sem=recv_sem.at[phase],
            device_id=device,
            device_id_type=MESH,
        ).start()

    def wait_bytes(like, semaphore):
        pltpu.make_async_copy(like, like, semaphore).wait()

    def each_col(body):
        for c in columns[1:]:
            body(c)

    def each_frame(body):
        for number in range(1, 4):
            body(lax.rem(frame + number, 4))

    def block(number, size):
        return pl.ds(pl.multiple_of(number * size, size), size)

    def send_partner(number):
        plane, a, part = number // 8, number // 4 % 2, number % 4
        rows = block(part, 64)
        source = (real_ref, imaginary_ref)[plane]
        send(source.at[2 + a, rows], partner.at[plane, a, rows], 3, mirror)

    each_col(
        lambda c: send(
            object_ref.at[8 * frame + c], object_rows.at[col], 0, (frame, row, c)
        )
    )
    for number in range(6):
        send_partner(number)
    for load in transfer_loads:
        load.wait()
    for plane in range(2):
        extra_send[plane] = transfer[plane, 0, pl.ds(0, 32, stride=8), :]
    def send_image(c):
        send(images_ref.at[pl.ds(4 * c, 4)], image_rows.at[col], 1, (frame, row, c))

    def field_of(read):
        return jnp.concatenate(
            [
                jnp.concatenate([read(x1 // 2, 2 * (x1 % 2) + part) for x1 in range(16)], 0)
                for part in range(2)
            ],
            1,
        )

    def to_all(source, target, size, phase):
        target[block(me, size), :] = source[block(me, size), :]
        own = block(me, size)
        each_peer(
            lambda r, c: send(
                source.at[block(r * 8 + c, size)], target.at[own], phase, (frame, r, c)
            )
        )

    object_load.wait()
    wait_bytes(object_rows.at[pl.ds(0, 7)], recv_sem.at[0])
    need("open_x", "twist_out", "across")
    planes = rows_to_half([field_of(lambda c, k: object_rows[c, k])], tab)[0]
    for plane in range(2):
        send_a[pl.ds(plane, 128, stride=2), :] = planes[plane]
    quarter = pencils.at[block(frame, 256)]
    quarter[block(me, 2), :] = send_a[block(me, 2), :]

    def send_pencil(r, c):
        send(send_a.at[block(r * 8 + c, 2)], quarter.at[block(me, 2)], 5, (frame, r, c))

    def some_rows(step, carry):
        for number in range(5):
            for c in columns:
                send_pencil(lax.rem(row + 1 + lax.rem(6 + 5 * step + number, 15), 16), c)
        return carry

    for c in columns[1:]:
        send_pencil(row, c)
    lax.fori_loop(0, 3, some_rows, 0)
    send(extra_send, extra, 2, after)
    for number in range(6, 16):
        send_partner(number)
        if number >= 9:
            send_image(columns[number - 8])
    wait_bytes(send_a.at[pl.ds(0, 254)], recv_sem.at[5])
    each_frame(lambda f: send(quarter, quarter, 7, (f, row, col)))
    wait_bytes(pencils.at[pl.ds(0, 768)], recv_sem.at[7])

    def turns(number):
        return (
            tab["twist_vertical"][pl.ds(128 * number, 128), :],
            tab["twist_vertical"][pl.ds(512 + 128 * number, 128), :],
        )

    def opened(name, number, rows):
        return table_first(
            tab[name][pl.ds(512 * number, 512), rows], split_high[rows], split_low[rows], product
        )

    def up(mixed, number, conjugate):
        rows = pl.ds(128 * number, 128)
        weights = [(weight[k, 0, rows, :], weight[k, 1, rows, :]) for k in range(3)]
        planes = up_chunk(mixed, *turns(number), tab, weights, conjugate)
        for plane, values in enumerate(planes):
            high, low = split(values)
            for which in range(2):
                part = slice(128 * which, 128 * which + 128)
                at = pl.ds(512 * plane + 128 * number, 128)
                back_high[which, at, :] = high[part]
                back_low[which, at, :] = low[part]

    for plane in range(2):
        high, low = split(pencils[pl.ds(plane, 512, stride=2), :])
        split_high[:, 128 * plane : 128 * plane + 128] = high
        split_low[:, 128 * plane : 128 * plane + 128] = low
    need("down_object", "twist_vertical", "mix_down")
    for number in range(4):
        middle[number] = down_chunk(
            opened("down_object", number, slice(0, 512)), *turns(number), tab
        )

    wait_bytes(extra, recv_sem.at[2])
    wait_bytes(partner, recv_sem.at[3])
    need("choose")
    kind = (me + 127) // 128 + me // 64
    for part in range(4):
        blocks = []
        for plane in range(2):
            rows = [
                transfer[plane, a, pl.ds((4 * v + part) * 8, 8), :]
                for a in range(4)
                for v in range(8)
            ]
            rows += [
                partner[plane, a, pl.ds((4 * v + part) * 8, 8), :]
                for a in range(2)
                for v in range(8)
            ]
            rows += [extra[plane, pl.ds(part, 8, stride=4), :], jnp.zeros((120, 128), F32)]
            blocks.append(jnp.concatenate(rows, 0))
        gathered = jnp.concatenate(blocks, 1)
        first = gathered.astype(BF16)
        left = gathered - first.astype(F32)
        second = left.astype(BF16)
        third = (left - second.astype(F32)).astype(BF16)
        chosen = tab["choose"][kind]
        picked = product(chosen, first) + (product(chosen, second) + product(chosen, third))
        for number in range(3):
            for plane in range(2):
                weight[number, plane, pl.ds(128 * part, 128), :] = picked[
                    128 * number : 128 * number + 128, 128 * plane : 128 * plane + 128
                ].T

    def return_chunk(name, number):
        table = tab[name][block(number, 256), :]
        real = table_first(table[:, 512:], back_high[0], back_low[0], product)
        imaginary = table_first(table[:, :1024], back_high[1], back_low[1], product)
        return real, imaginary

    need("mix_up")
    for number in range(4):
        up(middle[number], number, False)
    need("up_full")
    for half in range(2):
        for number in range(2):
            planes = return_chunk("up_full", 2 * half + number)
            for plane in range(2):
                send_four[half, pl.ds(2 * plane + number, 128, stride=4), :] = planes[plane]
        if half == 1:
            wait_bytes(got_four.at[0, pl.ds(0, 127 * 4)], send_sem.at[8])
        to_all(send_four.at[half], got_four.at[half], 4, 8 + half)

    images_load.wait()
    wait_bytes(image_rows.at[pl.ds(0, 7)], recv_sem.at[1])
    need("back_x", "twist_in", "close_x")
    for half in range(2):
        wait_bytes(got_four.at[half, pl.ds(0, 127 * 4)], recv_sem.at[8 + half])
        modelled = half_to_rows(
            [
                jnp.concatenate(
                    [
                        got_four[half, pl.ds(number, 128, stride=4), :],
                        got_four[half, pl.ds(2 + number, 128, stride=4), :],
                    ],
                    0,
                )
                for number in range(2)
            ],
            tab,
        )
        weighted = []
        for number, model in enumerate(modelled):
            images = field_of(lambda c, k: image_rows[c, 2 * half + number, k])
            weighted.append((model - images) / (0.5 + jnp.abs(images)))
        for number, planes in enumerate(rows_to_half(weighted, tab)):
            for plane in range(2):
                send_five[half, pl.ds(2 * plane + number, 128, stride=4), :] = planes[plane]
        to_all(send_five.at[half], got_five.at[half], 4, 14 + half)

    need("down_full", "up_gradient")
    for half in range(2):
        wait_bytes(got_five.at[half, pl.ds(0, 127 * 4)], recv_sem.at[14 + half])
        for plane in range(2):
            for number in range(2):
                high, low = split(got_five[half, pl.ds(2 * plane + number, 128, stride=4), :])
                first = 256 * half + 128 * number
                at = (slice(first, first + 128), slice(128 * plane, 128 * plane + 128))
                split_high[at] = high
                split_low[at] = low
        if half == 0:
            for number in range(4):
                middle[number] = opened("down_full", number, slice(0, 256))
    for number in range(4):
        whole = middle[number] + opened("down_full", number, slice(256, 512))
        up(down_chunk(whole, *turns(number), tab), number, True)

    near = row // 8
    parts = [block(near, 128), block(1 - near, 128)]
    for step in (2, 1, 3, 0):
        f = lax.rem(frame + step, 4)
        planes = return_chunk("up_gradient", f)
        target = got_six if step == 0 else send_six
        for plane in range(2):
            target[f, pl.ds(plane, 128, stride=2), :] = planes[plane]
        if step > 0:
            send(send_six.at[f, parts[0]], got_six.at[frame, parts[0]], 4, (f, row, col))
    for step in (2, 1, 3):
        f = lax.rem(frame + step, 4)
        send(send_six.at[f, parts[1]], got_six.at[frame, parts[1]], 10, (f, row, col))
    for half in range(2):
        wait_bytes(send_six.at[pl.ds(0, 3), pl.ds(0, 128)], recv_sem.at[4 if half == 0 else 10])
        pieces = [got_six[f, parts[half], :] for f in range(4)]
        send_c[parts[half], :] = (pieces[0] + pieces[1]) + (pieces[2] + pieces[3])
        first = 8 * near if half == 0 else 8 - 8 * near

        def send_quarter(r, c):
            send(send_c.at[block(r * 8 + c, 2)], got_d.at[block(me, 2)], 11, (frame, r, c))

        def some_rows(number, carry):
            for c in columns:
                send_quarter(first + lax.rem(row + number, 8), c)
            return carry

        if half == 0:
            got_d[block(me, 2), :] = send_c[block(me, 2), :]
            for c in columns[1:]:
                send_quarter(row, c)
        lax.fori_loop(1 - half, 8, some_rows, 0)
    wait_bytes(send_c.at[pl.ds(0, 254)], recv_sem.at[11])
    field = half_to_rows(
        [jnp.concatenate([got_d[pl.ds(0, 128, stride=2), :], got_d[pl.ds(1, 128, stride=2), :]], 0)],
        tab,
    )[0]
    for x1 in range(16):
        for part in range(2):
            send_out[x1 // 2, 2 * (x1 % 2) + part] = field[
                8 * x1 : 8 * x1 + 8, 128 * part : 128 * part + 128
            ]
    got_out[col] = send_out[col]
    each_col(lambda c: send(send_out.at[c], got_out.at[col], 13, (frame, row, c)))
    wait_bytes(send_out.at[pl.ds(0, 7)], recv_sem.at[13])
    out_ref[...] = got_out[...]

    wait_bytes(object_rows.at[pl.ds(0, 7)], send_sem.at[0])
    wait_bytes(image_rows.at[pl.ds(0, 7)], send_sem.at[1])
    wait_bytes(extra, send_sem.at[2])
    wait_bytes(partner, send_sem.at[3])
    wait_bytes(send_a.at[pl.ds(0, 254)], send_sem.at[5])
    wait_bytes(pencils.at[pl.ds(0, 768)], send_sem.at[7])
    wait_bytes(got_four.at[1, pl.ds(0, 127 * 4)], send_sem.at[9])
    for half in range(2):
        wait_bytes(got_five.at[half, pl.ds(0, 127 * 4)], send_sem.at[14 + half])
    wait_bytes(send_six.at[pl.ds(0, 3), pl.ds(0, 128)], send_sem.at[4])
    wait_bytes(send_six.at[pl.ds(0, 3), pl.ds(0, 128)], send_sem.at[10])
    wait_bytes(send_c.at[pl.ds(0, 254)], send_sem.at[11])
    wait_bytes(send_out.at[pl.ds(0, 7)], send_sem.at[13])


def tiles(block):
    rows, columns = block.shape
    return block.reshape(rows // 8, 8, columns // 128, 128).transpose(0, 2, 1, 3)


def shards(object_field, images, transfer_real, transfer_imaginary):
    made = tables()
    operands = [made[name] for name in NAMES]
    scratch = [pltpu.VMEM(table.shape, table.dtype) for table in operands]
    scratch += [
        pltpu.VMEM((2, 4, 256, 128), F32),
        pltpu.VMEM((2, 2, 256, 128), F32),
        pltpu.VMEM((2, 32, 128), F32),
        pltpu.VMEM((2, 32, 128), F32),
        pltpu.VMEM((8, 4, 8, 128), F32),
        pltpu.VMEM((8, 4, 4, 8, 128), F32),
        pltpu.VMEM((256, 128), F32),
        pltpu.VMEM((1024, 128), F32),
        pltpu.VMEM((4, 256, 256), F32),
        pltpu.VMEM((3, 2, 512, 128), F32),
        pltpu.VMEM((512, 256), BF16),
        pltpu.VMEM((512, 256), BF16),
        pltpu.VMEM((2, 1024, 128), BF16),
        pltpu.VMEM((2, 1024, 128), BF16),
        pltpu.VMEM((2, 512, 128), F32),
        pltpu.VMEM((2, 512, 128), F32),
        pltpu.VMEM((2, 512, 128), F32),
        pltpu.VMEM((2, 512, 128), F32),
        pltpu.VMEM((4, 256, 128), F32),
        pltpu.VMEM((4, 256, 128), F32),
        pltpu.VMEM((256, 128), F32),
        pltpu.VMEM((256, 128), F32),
        pltpu.VMEM((8, 4, 8, 128), F32),
        pltpu.VMEM((8, 4, 8, 128), F32),
        pltpu.SemaphoreType.DMA((len(NAMES),)),
        pltpu.SemaphoreType.DMA((4,)),
        pltpu.SemaphoreType.DMA((16,)),
        pltpu.SemaphoreType.DMA((16,)),
    ]
    anywhere = pl.BlockSpec(memory_space=pl.ANY)
    block = pl.pallas_call(
        kernel,
        out_shape=jax.ShapeDtypeStruct((8, 4, 8, 128), F32),
        in_specs=[anywhere] * (4 + len(NAMES)),
        out_specs=pl.BlockSpec(memory_space=pltpu.VMEM),
        scratch_shapes=scratch,
        compiler_params=pltpu.CompilerParams(
            collective_id=0, has_side_effects=True, vmem_limit_bytes=56 * 1024 * 1024
        ),
        name="gradient",
    )(
        tiles(object_field),
        tiles(images[0]),
        tiles(transfer_real[0]).reshape(4, 256, 128),
        tiles(transfer_imaginary[0]).reshape(4, 256, 128),
        *operands,
    )
    return block.transpose(0, 2, 1, 3).reshape(64, 512)


def solution(mesh):
    placed = (
        P("row", "col"),
        P("frame", "row", "col"),
        P("frame", ("row", "col"), None),
        P("frame", ("row", "col"), None),
    )
    return jax.shard_map(
        shards, mesh=mesh, in_specs=placed, out_specs=P(("frame", "row"), "col"), check_vma=False
    )
```
